128 devices in a mesh: text: 8 (over y, core), graph: 16 (over x, z).
Axes of the slice: x: 4, y: 4, z: 4, core: 2. Of those that a mesh axis runs over, the one named last changes fastest.
Arguments:
- states: bfloat16 [512, 64, 768], P(('text', 'graph')), may hold values from -6 to 6
- weight_in: bfloat16 [3072, 768], P(('text', 'graph')), may hold values from -0.21875 to 0.21875
- weight_out: bfloat16 [3072, 768], P(('text', 'graph')), may hold values from -0.109375 to 0.109375
- node_table: bfloat16 [131072, 768], P(('text', 'graph')), may hold values from -6 to 6
- adjacency: bfloat16 [1024, 4, 128, 128], P(('text', 'graph')), may hold values from -0.25 to 0.25
- sources: int32 [1024, 4], P(('text', 'graph')), may hold values from 0 to 11
- node_ids: int32 [512], replicated, may hold values from 0 to 131071, as said below
- self_first: bfloat16 [768, 256], replicated, may hold values from -0.21875 to 0.21875
- neigh_first: bfloat16 [768, 256], replicated, may hold values from -0.21875 to 0.21875
- self_second: bfloat16 [256, 256], replicated, may hold values from -0.375 to 0.375
- neigh_second: bfloat16 [256, 256], replicated, may hold values from -0.375 to 0.375
- upstream: bfloat16 [131072, 256], P(('text', 'graph')), may hold values from -6 to 6
Outputs:
- gnn_out: bfloat16 [131072, 256], P(('text', 'graph'))
- table_grad: float32 [131072, 768], P(('text', 'graph'))
- node_grad: float32 [512, 768], P(('text', 'graph'))
- grad_in: float32 [3072, 768], P(('text', 'graph'))
- grad_out: float32 [3072, 768], P(('text', 'graph'))
- grad_self_first: float32 [768, 256], replicated
- grad_neigh_first: float32 [768, 256], replicated
- grad_self_second: float32 [256, 256], replicated
- grad_neigh_second: float32 [256, 256], replicated
The draws below stay inside these ranges and needn't reach their ends.
Inputs may be any that keep to these rules, and one draw needn't show every extreme that they name: `node_ids`: distinct rows.
All inputs are finite; a program needn't handle non-finite values.
Results may differ from the reference program's by a relative error of at most 0.009.
Values may be sent and summed in bfloat16 or wider, within the bound.
A program may use at most 128 MiB of HBM per device.

```python
import math
import jax
import jax.numpy as jnp
from jax import lax

D = 768
FFH = 3072
HID = 256
SEQ = 64
BLK = 128
TILES = 4
BND = 2
ROWS_DEV = 1024
NFT = 512
NODES = 131072
N_GRAPH = 16


def draw_node_ids(key, part):
    key = jax.random.fold_in(key, 7)
    return jax.random.permutation(key, NODES)[:NFT].astype(jnp.int32)


def with_ends(values, own_key, smallest, largest):
    longest = values.shape.index(max(values.shape))
    spots = []
    for shift in (0, 1):
        where = [jax.random.randint(jax.random.fold_in(own_key, axis), (), 0, length) for axis, length in enumerate(values.shape)]
        where[longest] = (where[longest] + shift) % values.shape[longest]
        spots.append(tuple(where))
    return values.at[spots[0]].set(smallest).at[spots[1]].set(largest)


def shard_levels(own_key, dims, cuts, least, largest):
    loudness, own = 1.0, jax.random.fold_in(own_key, 6)
    for axis_at, parts in cuts:
        draws = jnp.exp(jax.random.uniform(jax.random.fold_in(own, axis_at), (parts,), jnp.float32, least / len(cuts), largest / len(cuts)))
        loudness = loudness * jnp.repeat(draws, dims[axis_at] // parts).reshape([-1 if axis == axis_at else 1 for axis in range(len(dims))])
    return loudness


def bell_draw(own_key, dims, width, limit, cuts=(), held_as=jnp.bfloat16):
    gain = shard_levels(own_key, dims, cuts, -0.22, 0.18) if cuts else 1.0
    values = jax.random.normal(own_key, dims, jnp.float32) * width * gain
    return jnp.minimum(jnp.maximum(values, -limit), limit).astype(held_as)


def setup_inputs(seed: int = 0) -> dict:
    keys = jax.random.split(jax.random.key(seed), 13)
    return {
        "states": bell_draw(keys[0], (NFT, SEQ, D), 1.0, 6.0, ((0, 128),)),
        "weight_in": bell_draw(keys[1], (FFH, D), D ** -0.5, 0.21875, ((0, 128),)),
        "weight_out": bell_draw(keys[2], (FFH, D), FFH ** -0.5, 0.109375, ((0, 128),)),
        "node_table": bell_draw(keys[3], (NODES, D), 1.0, 6.0, ((0, 128),)),
        "adjacency": bell_draw(keys[4], (NODES // BLK, TILES, BLK, BLK), (BLK * TILES) ** -0.5, 0.25, ((0, 128),)),
        "sources": with_ends(jax.random.randint(keys[5], (NODES // BLK, TILES), 0, ROWS_DEV // BLK + 2 * BND), jax.random.fold_in(keys[5], 1), 0, (ROWS_DEV // BLK + 2 * BND) - 1).astype(jnp.int32),
        "node_ids": draw_node_ids(jax.random.fold_in(keys[12], 71), 0),
        "self_first": bell_draw(keys[7], (D, HID), D ** -0.5, 0.21875),
        "neigh_first": bell_draw(keys[8], (D, HID), D ** -0.5, 0.21875),
        "self_second": bell_draw(keys[9], (HID, HID), HID ** -0.5, 0.375),
        "neigh_second": bell_draw(keys[10], (HID, HID), HID ** -0.5, 0.375),
        "upstream": bell_draw(keys[11], (NODES, HID), 1.0, 6.0, ((0, 128),)),
    }


precise = lax.Precision.HIGHEST

def gelu_value(values):
    return 0.5 * values * (1.0 + jax.scipy.special.erf(values * (1.0 / math.sqrt(2.0))))

def gelu_slope(values):
    normal_cdf = 0.5 * (1.0 + jax.scipy.special.erf(values * (1.0 / math.sqrt(2.0))))
    return normal_cdf + values * jnp.exp(-0.5 * values * values) * (1.0 / math.sqrt(2.0 * math.pi))

def global_sources(sources):
    local_blocks = ROWS_DEV // BLK
    device = jnp.arange(NODES // BLK, dtype=jnp.int32) // local_blocks
    text_index = device // N_GRAPH
    graph_index = device % N_GRAPH
    below = text_index * N_GRAPH + (graph_index + N_GRAPH - 1) % N_GRAPH
    above = text_index * N_GRAPH + (graph_index + 1) % N_GRAPH
    lower = below[:, None] * local_blocks + local_blocks - BND + sources
    middle = device[:, None] * local_blocks + sources - BND
    upper = above[:, None] * local_blocks + sources - BND - local_blocks
    chosen = jnp.where(sources < BND, lower, jnp.where(sources < BND + local_blocks, middle, upper))
    return chosen.astype(jnp.int32)

def aggregate(values, adjacency, source_blocks):
    wide = values.shape[1]
    blocks = values.reshape(NODES // BLK, BLK, wide)

    def one_block(block_args):
        tile_set, picked = block_args
        gathered = jnp.take(blocks, picked, axis=0)
        return jnp.einsum('tij,tjw->iw', tile_set.astype(jnp.float32), gathered, precision=precise)
    result = lax.map(one_block, (adjacency, source_blocks))
    return result.reshape(NODES, wide)

def aggregate_back(values, adjacency, source_blocks):
    wide = values.shape[1]
    blocks = values.reshape(NODES // BLK, BLK, wide).astype(jnp.float32)

    def add_tile(running, tile_index):
        tile_set = lax.dynamic_index_in_dim(adjacency, tile_index, 1, keepdims=False).astype(jnp.float32)
        picked = lax.dynamic_index_in_dim(source_blocks, tile_index, 1, keepdims=False)
        terms = jnp.einsum('bij,biw->bjw', tile_set, blocks, precision=precise)
        return (running + jax.ops.segment_sum(terms, picked, num_segments=NODES // BLK), None)
    start_sum = jnp.zeros((NODES // BLK, BLK, wide), jnp.float32)
    running = lax.scan(add_tile, start_sum, jnp.arange(TILES))[0]
    return running.reshape(NODES, wide)

def reference(states, weight_in, weight_out, node_table, adjacency, sources, node_ids, self_first, neigh_first, self_second, neigh_second, upstream):
    wide_states = states.astype(jnp.float32)
    row_mean = lax.optimization_barrier(jnp.mean(wide_states, axis=-1, keepdims=True))
    centered = wide_states - row_mean
    variance = lax.optimization_barrier(jnp.mean(centered * centered, axis=-1, keepdims=True))
    normed = (centered * lax.rsqrt(variance + 1e-05)).astype(jnp.bfloat16).reshape(NFT * SEQ, D)
    before = jnp.dot(normed, weight_in.T, preferred_element_type=jnp.float32)
    active = gelu_value(before).astype(jnp.bfloat16)
    mixed_rows = states.reshape(NFT * SEQ, D).astype(jnp.float32) + jnp.dot(active, weight_out, preferred_element_type=jnp.float32)
    embedded = lax.optimization_barrier(jnp.mean(mixed_rows.reshape(NFT, SEQ, D), axis=1)).astype(jnp.bfloat16)
    features = node_table.at[node_ids].set(embedded)
    source_blocks = global_sources(sources)
    first_proj = jnp.dot(features, neigh_first, preferred_element_type=jnp.float32)
    first_pre = jnp.dot(features, self_first, preferred_element_type=jnp.float32) + aggregate(first_proj, adjacency, source_blocks)
    hidden = gelu_value(first_pre).astype(jnp.bfloat16)
    second_proj = jnp.dot(hidden, neigh_second, preferred_element_type=jnp.float32)
    second_pre = jnp.dot(hidden, self_second, preferred_element_type=jnp.float32) + aggregate(second_proj, adjacency, source_blocks)
    gnn_out = second_pre.astype(jnp.bfloat16)
    node_scale = 1.0 / math.sqrt(NODES)
    back_second = aggregate_back(upstream, adjacency, source_blocks).astype(jnp.bfloat16)
    grad_self_second = jnp.dot(hidden.T, upstream, preferred_element_type=jnp.float32) * node_scale
    grad_neigh_second = jnp.dot(hidden.T, back_second, preferred_element_type=jnp.float32) * node_scale
    hidden_grad = jnp.dot(upstream, self_second.T, preferred_element_type=jnp.float32) + jnp.dot(back_second, neigh_second.T, preferred_element_type=jnp.float32)
    first_grad = (hidden_grad * gelu_slope(first_pre)).astype(jnp.bfloat16)
    back_first = aggregate_back(first_grad, adjacency, source_blocks).astype(jnp.bfloat16)
    grad_self_first = jnp.dot(features.T, first_grad, preferred_element_type=jnp.float32) * node_scale
    grad_neigh_first = jnp.dot(features.T, back_first, preferred_element_type=jnp.float32) * node_scale
    table_grad = jnp.dot(first_grad, self_first.T, preferred_element_type=jnp.float32) + jnp.dot(back_first, neigh_first.T, preferred_element_type=jnp.float32)
    node_grad = table_grad[node_ids]
    token_grad = jnp.broadcast_to((node_grad / SEQ)[:, None, :], (NFT, SEQ, D)).astype(jnp.bfloat16).reshape(NFT * SEQ, D)
    adjusted_scale = 1.0 / math.sqrt(NFT)
    grad_out = jnp.dot(active.T, token_grad, preferred_element_type=jnp.float32) * adjusted_scale
    act_grad = jnp.dot(token_grad, weight_out.T, preferred_element_type=jnp.float32)
    pre_grad = (act_grad * gelu_slope(before)).astype(jnp.bfloat16)
    grad_in = jnp.dot(pre_grad.T, normed, preferred_element_type=jnp.float32) * adjusted_scale
    return (gnn_out, table_grad, node_grad, grad_in, grad_out, grad_self_first, grad_neigh_first, grad_self_second, grad_neigh_second)
```

```python
import math
from types import SimpleNamespace

import jax
import jax.numpy as jnp
from jax import lax
from jax.experimental import pallas as pl
from jax.experimental.pallas import tpu as pltpu
from jax.sharding import PartitionSpec as P

MESH = pl.DeviceIdType.MESH
F32 = jnp.float32
BF16 = jnp.bfloat16

D = 768
FFH = 3072
HID = 256
SEQ = 64
ROWS = 1024
RIM = 256
EXT = ROWS + 2 * RIM
NFT = 512
NG = 16
NT = 8
CHUNK = FFH // NT
OWN = FFH // (NT * NG)
NODE_SCALE = 1.0 / math.sqrt(131072)
TEXT_SCALE = 1.0 / math.sqrt(NFT)

INPUTS = (
    "states", "w_in", "w_out", "table", "adj", "src", "ids",
    "sf", "nf", "ss", "ns", "ups",
)
OUTPUTS = {
    "gnn": ((ROWS, HID), BF16),
    "tgrad": ((ROWS, D), F32),
    "ngrad": ((4, D), F32),
    "gin": ((OWN, D), F32),
    "gout": ((OWN, D), F32),
    "gsf": ((D, HID), F32),
    "gnf": ((D, HID), F32),
    "gss": ((HID, HID), F32),
    "gns": ((HID, HID), F32),
}
SCRATCH = {
    "wpack": ((NG, 2 * OWN, D), BF16),
    "wide_in": ((CHUNK, D), F32),
    "wide_out": ((CHUNK, D), F32),
    "wi": ((CHUNK, D), BF16),
    "wo": ((CHUNK, D), BF16),
    "normed": ((NT, 256, D), BF16),
    "smean": ((8, D), F32),
    "before": ((256, CHUNK), F32),
    "slope": ((NT, 256, CHUNK), F32),
    "asum": ((32, CHUNK), F32),
    "part": ((32, D), F32),
    "part2": ((2, 16, D), F32),
    "pairin": ((16, D), F32),
    "yemb": ((4, 16, D), BF16),
    "emb": ((2, NG, 16, D), BF16),
    "oh": ((EXT, NFT), BF16),
    "oht": ((NFT, EXT), BF16),
    "keep": ((EXT, 1), F32),
    "e": ((ROWS, EXT), BF16),
    "et": ((EXT, ROWS), BF16),
    "b2": ((EXT, HID), F32),
    "b2out": ((2, RIM, HID), BF16),
    "b2in": ((2, RIM, HID), BF16),
    "back2": ((ROWS, HID), BF16),
    "hg": ((ROWS, HID), F32),
    "tself": ((ROWS, HID), F32),
    "tn": ((EXT, HID), BF16),
    "pn": ((EXT, HID), BF16),
    "embproj": ((NFT, 2 * HID), BF16),
    "hid": ((EXT, HID), BF16),
    "proj2": ((EXT, HID), BF16),
    "fb": ((ROWS, 2 * HID), BF16),
    "b1": ((EXT, HID), F32),
    "b1b": ((EXT, HID), BF16),
    "b1in": ((2, RIM, HID), BF16),
    "feat": ((ROWS, D), BF16),
    "wg": ((2, 4, NG, 16, HID), BF16),
    "wgin": ((4, NG, 16, HID), BF16),
    "wg1": ((4, NG, 16, HID), BF16),
    "wgy": ((4, NG, 16, HID), BF16),
    "wg2": ((NG, 16, HID), BF16),
    "wgg": ((NG, 16, HID), BF16),
    "wgall": ((2, 4, NG, 16, HID), BF16),
    "pick": ((2, NG, 16, 2 * HID), BF16),
    "pickin": ((NG, 16, 2 * HID), BF16),
    "pick1": ((NG, 16, 2 * HID), BF16),
    "pickg": ((NG, 16, 2 * HID), BF16),
    "picky": ((4, 16, 2 * HID), BF16),
    "pickall": ((2, 16, 2 * HID), BF16),
    "nodeg": ((32, D), F32),
    "act": ((32, CHUNK), F32),
    "pre": ((NT, 256, CHUNK), BF16),
    "gfull": ((2, CHUNK, D), F32),
    "gpack": ((NG, 2 * OWN, D), BF16),
    "grecv": ((NG, 2 * OWN, D), BF16),
}
SEMS = {
    "w": 16, "st": 9, "rim": 8, "pair": 1, "ye": 4, "eg": 16, "es": 16,
    "pk": 1, "pg": 16, "py": 4, "ps": 1,
    "a1": 1, "a2": 4, "a3": 16, "a4": 16, "a5": 4, "a6": 1, "gr": 16,
}


def dot(a, b):
    return jnp.dot(a, b, preferred_element_type=F32)


def dot_nt(a, b):
    return lax.dot_general(a, b, (((1,), (1,)), ((), ())), preferred_element_type=F32)


def dot_tn(a, b):
    return lax.dot_general(a, b, (((0,), (0,)), ((), ())), preferred_element_type=F32)


def gelu_pair(v):
    cdf = 0.5 * (1.0 + lax.erf(v * (1.0 / math.sqrt(2.0))))
    return v * cdf, cdf + v * jnp.exp(-0.5 * v * v) * (1.0 / math.sqrt(2.0 * math.pi))


def split(v):
    high = v.astype(BF16)
    return high, (v - high.astype(F32)).astype(BF16)


def body(*refs):
    names = list(INPUTS) + list(OUTPUTS) + list(SCRATCH)
    r = SimpleNamespace(**dict(zip(names, refs)))
    sems = {}
    at = len(names)
    for name in SEMS:
        sems[name] = (refs[at], refs[at + 1])
        at += 2

    t = lax.axis_index("text")
    g = lax.axis_index("graph")
    c = lax.rem(t, 2)
    y = lax.div(t, 2)
    sib = t + 1 - 2 * c

    def at_y(step):
        return lax.rem(y + step, 4) * 2 + c

    up, opp, down = at_y(1), at_y(2), at_y(3)
    ahead = lax.rem(g + 1, NG)
    behind = lax.rem(g + NG - 1, NG)
    pending = []

    def send(src, dst, kind, tag, to, start=True):
        copy = pltpu.make_async_remote_copy(
            src_ref=src, dst_ref=dst, send_sem=sems[kind][0].at[tag],
            recv_sem=sems[kind][1].at[tag], device_id=to, device_id_type=MESH,
        )
        if start:
            copy.start()
            pending.append(copy)
        return copy

    def arrived(dst, kind, tag):
        send(dst, dst, kind, tag, (sib, g), start=False).wait_recv()

    def each_peer(fn):
        def step(k, carry):
            fn(k, lax.rem(g + k, NG), lax.rem(g + NG - k, NG))
            return carry

        lax.fori_loop(1, NG, step, 0)

    def scatter(src_of, dst, kind):
        def one(k, to, source):
            pltpu.make_async_remote_copy(
                src_ref=src_of(to), dst_ref=dst.at[g], send_sem=sems[kind][0].at[k],
                recv_sem=sems[kind][1].at[k], device_id=(t, to), device_id_type=MESH,
            ).start()

        each_peer(one)

    def scatter_wait(dst, kind):
        each_peer(lambda k, to, source: arrived(dst.at[source], kind, k))

    def scatter_sent(src, kind):
        def one(k, to, source):
            send(src, src, kind, k, (t, to), start=False).wait_send()

        each_peer(one)

    barrier = pltpu.get_barrier_semaphore()

    def greet(to):
        pl.semaphore_signal(barrier, inc=1, device_id=to, device_id_type=MESH)

    for peer in (sib, up, opp, down):
        greet((peer, g))
    each_peer(lambda k, to, source: greet((t, to)))
    pl.semaphore_wait(barrier, 19)

    both = jnp.concatenate([r.w_in[...].astype(F32), r.w_out[...].astype(F32)], axis=0)
    r.wpack[g] = both.astype(BF16)
    scatter(lambda to: r.wpack.at[g], r.wpack, "w")

    for i in range(4):
        x = r.states[i * SEQ : (i + 1) * SEQ, :].astype(F32)
        r.smean[i : i + 1, :] = jnp.sum(x, axis=0, keepdims=True) * (1.0 / SEQ)
        mean = jnp.mean(x, axis=1, keepdims=True)
        centered = x - mean
        var = jnp.mean(centered * centered, axis=1, keepdims=True)
        r.normed[t, i * SEQ : (i + 1) * SEQ, :] = (centered * lax.rsqrt(var + 1e-05)).astype(BF16)
    mine = r.normed.at[t]
    send(mine, mine, "st", 0, (sib, g))
    send(mine, mine, "st", 1, (up, g))
    send(mine, mine, "st", 2, (down, g))

    for i in (0, 3, 1, 2):
        rows = slice(i * 256, (i + 1) * 256)
        x = r.table[rows, :]
        r.tn[RIM + i * 256 : RIM + (i + 1) * 256, :] = dot(x, r.nf[...]).astype(BF16)
        r.tself[rows, :] = dot(x, r.sf[...])
        if i == 3:
            send(r.tn.at[RIM : 2 * RIM], r.tn.at[RIM + ROWS :], "rim", 0, (t, behind))
            send(r.tn.at[ROWS : ROWS + RIM], r.tn.at[:RIM], "rim", 1, (t, ahead))

    def tiles(b, carry):
        rows = pl.ds(pl.multiple_of(b * 128, 128), 128)
        plain = [r.adj[b * 4 + k] for k in range(4)]
        turned = [p.astype(F32).T.astype(BF16) for p in plain]
        for s in range(12):
            own = jnp.zeros((128, 128), BF16)
            other = jnp.zeros((128, 128), BF16)
            for k in range(4):
                hit = r.src[b, k] == s
                own = own + jnp.where(hit, plain[k], jnp.zeros_like(plain[k]))
                other = other + jnp.where(hit, turned[k], jnp.zeros_like(turned[k]))
            r.e[rows, s * 128 : (s + 1) * 128] = own
            r.et[s * 128 : (s + 1) * 128, rows] = other
        return carry

    lax.fori_loop(0, 8, tiles, 0)

    for i in (0, 5, 1, 2, 3, 4):
        rows = slice(i * 256, (i + 1) * 256)
        r.b2[rows, :] = dot(r.et[rows, :], r.ups[...])
        if i == 5:
            r.b2out[0] = r.b2[:RIM, :].astype(BF16)
            r.b2out[1] = r.b2[RIM + ROWS :, :].astype(BF16)
            send(r.b2out.at[0], r.b2in.at[1], "rim", 2, (t, behind))
            send(r.b2out.at[1], r.b2in.at[0], "rim", 3, (t, ahead))

    row = lax.broadcasted_iota(jnp.int32, (NFT, NFT), 0)
    col = lax.broadcasted_iota(jnp.int32, (NFT, NFT), 1)
    wanted = (col & 256) + ((col >> 2) & 3) * 64 + ((col >> 4) & 15) * 4 + (col & 3)
    moved = jnp.where(row == wanted, 1.0, 0.0).astype(BF16)
    ids = jnp.broadcast_to(r.ids[...], (8, NFT))
    pieces = [((ids >> shift) & 63).astype(F32).astype(BF16) for shift in (0, 6, 12)]
    low, middle, high = [dot(p, moved) for p in pieces]
    spot = low + 64.0 * middle + 4096.0 * high
    spot_row = spot[:1, :]
    spot_col = jnp.broadcast_to(spot_row, (128, NFT)).T
    device = t * NG + g
    starts = [(t * NG + behind) * ROWS + 768 + e * 128 for e in range(2)]
    starts += [device * ROWS + e * 128 for e in range(8)]
    starts += [(t * NG + ahead) * ROWS + e * 128 for e in range(2)]
    for e in range(12):
        start = starts[e].astype(F32)
        down_rows = lax.broadcasted_iota(jnp.int32, (128, NFT), 0).astype(F32) + start
        hit = jnp.where(down_rows == spot_row, 1.0, 0.0)
        r.oh[e * 128 : (e + 1) * 128, :] = hit.astype(BF16)
        r.keep[e * 128 : (e + 1) * 128, :] = 1.0 - jnp.sum(hit, axis=1, keepdims=True)
        across = lax.broadcasted_iota(jnp.int32, (NFT, 128), 1).astype(F32) + start
        r.oht[:, e * 128 : (e + 1) * 128] = jnp.where(across == spot_col, 1.0, 0.0).astype(BF16)

    scatter_wait(r.wpack, "w")

    def unpack(k, carry):
        block = r.wpack[k].astype(F32)
        rows = pl.ds(pl.multiple_of(k * OWN, 8), OWN)
        r.wide_in[rows, :] = block[:OWN]
        r.wide_out[rows, :] = block[OWN:]
        return carry

    lax.fori_loop(0, NG, unpack, 0)
    r.wi[...] = r.wide_in[...].astype(BF16)
    r.wo[...] = r.wide_out[...].astype(BF16)

    def encode(slot):
        r.before[...] = dot_nt(r.normed[slot], r.wi[...])

        def node(i, carry):
            rows = pl.ds(pl.multiple_of(i * SEQ, SEQ), SEQ)
            value, slope = gelu_pair(r.before[rows, :])
            r.slope[slot, rows, :] = slope
            r.asum[pl.ds(slot * 4 + i, 1), :] = jnp.sum(value, axis=0, keepdims=True)
            return carry

        lax.fori_loop(0, 4, node, 0)

    def fellow(slot):
        return slot + 1 - 2 * c

    encode(t)
    from_down, from_up, far = r.normed.at[down], r.normed.at[up], r.normed.at[opp]
    arrived(from_down, "st", 1)
    send(from_down.at[:128], from_down.at[:128], "st", 3, (up, g))
    send(from_down, from_down, "st", 5, (sib, g))
    arrived(from_up, "st", 2)
    send(from_up.at[128:], from_up.at[128:], "st", 4, (down, g))
    send(from_up, from_up, "st", 6, (sib, g))
    arrived(r.normed.at[sib], "st", 0)
    encode(sib)
    encode(down)
    encode(up)
    arrived(far.at[:128], "st", 3)
    send(far.at[:128], far.at[:128], "st", 7, (sib, g))
    arrived(far.at[128:], "st", 4)
    send(far.at[128:], far.at[128:], "st", 8, (sib, g))
    arrived(r.normed.at[fellow(down)], "st", 5)
    encode(fellow(down))
    arrived(r.normed.at[fellow(up)], "st", 6)
    encode(fellow(up))
    encode(opp)
    far_pair = r.normed.at[fellow(opp)]
    arrived(far_pair.at[:128], "st", 7)
    arrived(far_pair.at[128:], "st", 8)
    encode(fellow(opp))

    a_high, a_low = split(r.asum[...] * (1.0 / SEQ))
    r.part[...] = dot(a_high, r.wo[...]) + dot(a_low, r.wo[...])
    for i in range(4):
        spot_rows = pl.ds(t * 4 + i, 1)
        r.part[spot_rows, :] = r.part[spot_rows, :] + r.smean[i : i + 1, :]
    r.part2[0] = r.part[:16, :]
    r.part2[1] = r.part[16:, :]
    send(r.part2.at[1 - c], r.pairin, "pair", 0, (sib, g))
    arrived(r.pairin, "pair", 0)
    r.yemb[y] = (r.part2[c] + r.pairin[...]).astype(BF16)
    for step, peer in ((1, up), (2, opp), (3, down)):
        send(r.yemb.at[y], r.yemb.at[y], "ye", step, (peer, g))
    for step in (1, 2, 3):
        arrived(r.yemb.at[lax.rem(y + 4 - step, 4)], "ye", step)
    total = r.yemb[0].astype(F32) + r.yemb[1].astype(F32)
    total = total + r.yemb[2].astype(F32) + r.yemb[3].astype(F32)
    r.emb[c, g] = total.astype(BF16)

    def emb_out(k, to, source):
        ref = r.emb.at[c, g]
        send(ref, ref, "eg", k, (t, to), start=False).start()

    each_peer(emb_out)
    own_emb = r.emb.at[c, g]
    send(own_emb, own_emb, "es", 0, (sib, g))

    arrived(r.b2in.at[0], "rim", 3)
    arrived(r.b2in.at[1], "rim", 2)
    r.b2[RIM : 2 * RIM, :] = r.b2[RIM : 2 * RIM, :] + r.b2in[0].astype(F32)
    r.b2[ROWS : ROWS + RIM, :] = r.b2[ROWS : ROWS + RIM, :] + r.b2in[1].astype(F32)
    r.back2[...] = r.b2[RIM : RIM + ROWS, :].astype(BF16)
    for i in range(4):
        rows = slice(i * 256, (i + 1) * 256)
        r.hg[rows, :] = dot_nt(r.ups[rows, :], r.ss[...]) + dot_nt(r.back2[rows, :], r.ns[...])
    arrived(r.tn.at[RIM + ROWS :], "rim", 0)
    arrived(r.tn.at[:RIM], "rim", 1)

    def emb_on(k, to, source):
        ref = r.emb.at[c, source]
        arrived(ref, "eg", k)
        send(ref, ref, "es", k, (sib, g), start=False).start()

    each_peer(emb_on)
    arrived(r.emb.at[1 - c, g], "es", 0)
    each_peer(lambda k, to, source: arrived(r.emb.at[1 - c, source], "es", k))

    emb_all = r.emb[...].reshape(NFT, D)
    r.embproj[:, :HID] = dot(emb_all, r.sf[...]).astype(BF16)
    r.embproj[:, HID:] = dot(emb_all, r.nf[...]).astype(BF16)
    for i in range(6):
        rows = slice(i * 256, (i + 1) * 256)
        new = dot(r.oh[rows, :], r.embproj[:, HID:])
        r.pn[rows, :] = (r.tn[rows, :].astype(F32) * r.keep[rows, :] + new).astype(BF16)

    for i in range(4):
        rows = slice(i * 256, (i + 1) * 256)
        ext = slice(RIM + i * 256, RIM + (i + 1) * 256)
        pre = r.tself[rows, :] * r.keep[ext, :] + dot(r.oh[ext, :], r.embproj[:, :HID])
        pre = pre + dot(r.e[rows, :], r.pn[...])
        value, slope = gelu_pair(pre)
        r.hid[ext, :] = value.astype(BF16)
        r.fb[rows, :HID] = (r.hg[rows, :] * slope).astype(BF16)
    send(r.hid.at[RIM : 2 * RIM], r.hid.at[RIM + ROWS :], "rim", 4, (t, behind))
    send(r.hid.at[ROWS : ROWS + RIM], r.hid.at[:RIM], "rim", 5, (t, ahead))
    for i in (0, 5, 1, 2, 3, 4):
        rows = slice(i * 256, (i + 1) * 256)
        term = dot(r.et[rows, :], r.fb[:, :HID])
        r.b1[rows, :] = term
        r.b1b[rows, :] = term.astype(BF16)
    send(r.b1b.at[:RIM], r.b1in.at[1], "rim", 6, (t, behind))
    send(r.b1b.at[RIM + ROWS :], r.b1in.at[0], "rim", 7, (t, ahead))

    for i in range(2):
        rows = slice(i * 256, (i + 1) * 256)
        first = dot(r.oht[rows, RIM : RIM + ROWS], r.fb[:, :HID]).astype(BF16)
        back = dot(r.oht[rows, :], r.b1b[...]).astype(BF16)
        r.pick[i, :, :, :HID] = first.reshape(NG, 16, HID)
        r.pick[i, :, :, HID:] = back.reshape(NG, 16, HID)
    send(r.pick.at[1 - c], r.pickin, "pk", 0, (sib, g))

    def features(i):
        rows = slice(i * 256, (i + 1) * 256)
        ext = slice(RIM + i * 256, RIM + (i + 1) * 256)
        old = r.table[rows, :].astype(F32) * r.keep[ext, :]
        r.feat[rows, :] = (old + dot(r.oh[ext, :], emb_all)).astype(BF16)

    features(0)
    features(1)
    arrived(r.pickin, "pk", 0)
    r.pick1[...] = (r.pick[c].astype(F32) + r.pickin[...].astype(F32)).astype(BF16)
    r.pickg[g] = r.pick1[g]
    scatter(lambda to: r.pick1.at[to], r.pickg, "pg")
    features(2)
    features(3)

    arrived(r.b1in.at[0], "rim", 7)
    arrived(r.b1in.at[1], "rim", 6)
    r.b1[RIM : 2 * RIM, :] = r.b1[RIM : 2 * RIM, :] + r.b1in[0].astype(F32)
    r.b1[ROWS : ROWS + RIM, :] = r.b1[ROWS : ROWS + RIM, :] + r.b1in[1].astype(F32)
    r.fb[:, HID:] = r.b1[RIM : RIM + ROWS, :].astype(BF16)

    for side in range(2):
        cols = slice(side * HID, (side + 1) * HID)
        for q in range(3):
            term = dot_tn(r.feat[:, q * 256 : (q + 1) * 256], r.fb[:, cols])
            r.wg[side, q] = (term * NODE_SCALE).astype(BF16).reshape(NG, 16, HID)
    hidden = r.hid[RIM : RIM + ROWS, :]
    r.wg[0, 3] = (dot_tn(hidden, r.ups[...]) * NODE_SCALE).astype(BF16).reshape(NG, 16, HID)
    r.wg[1, 3] = (dot_tn(hidden, r.back2[...]) * NODE_SCALE).astype(BF16).reshape(NG, 16, HID)
    send(r.wg.at[1 - c], r.wgin, "a1", 0, (sib, g))

    scatter_wait(r.pickg, "pg")
    mixed = r.pickg[0].astype(F32)
    for k in range(1, NG):
        mixed = mixed + r.pickg[k].astype(F32)
    r.picky[y] = mixed.astype(BF16)
    for step, peer in ((1, up), (2, opp), (3, down)):
        send(r.picky.at[y], r.picky.at[y], "py", step, (peer, g))

    for i in range(4):
        rows = slice(i * 256, (i + 1) * 256)
        r.tgrad[rows, :] = dot_nt(r.fb[rows, :HID], r.sf[...]) + dot_nt(r.fb[rows, HID:], r.nf[...])

    for step in (1, 2, 3):
        arrived(r.picky.at[lax.rem(y + 4 - step, 4)], "py", step)
    mixed = r.picky[0].astype(F32) + r.picky[1].astype(F32)
    mixed = mixed + r.picky[2].astype(F32) + r.picky[3].astype(F32)
    r.pickall[c] = mixed.astype(BF16)
    send(r.pickall.at[c], r.pickall.at[c], "ps", 0, (sib, g))

    arrived(r.wgin, "a1", 0)
    r.wg1[...] = (r.wg[c].astype(F32) + r.wgin[...].astype(F32)).astype(BF16)
    r.wgy[y] = r.wg1[y]
    for step, peer_y in ((1, lax.rem(y + 1, 4)), (2, lax.rem(y + 2, 4)), (3, lax.rem(y + 3, 4))):
        send(r.wg1.at[peer_y], r.wgy.at[y], "a2", step, (peer_y * 2 + c, g))

    arrived(r.pickall.at[1 - c], "ps", 0)
    rows32 = r.pickall[...].reshape(32, 2 * HID)
    node_grad = dot_nt(rows32[:, :HID], r.sf[...]) + dot_nt(rows32[:, HID:], r.nf[...])
    r.nodeg[...] = node_grad
    for i in range(4):
        r.ngrad[i : i + 1, :] = r.nodeg[pl.ds(t * 4 + i, 1), :]
    small = (node_grad * (1.0 / SEQ)).astype(BF16)
    r.act[...] = dot_nt(small, r.wo[...])

    def pre_grad(n, carry):
        slot = n // 4
        rows = pl.ds(pl.multiple_of((n % 4) * SEQ, SEQ), SEQ)
        r.pre[slot, rows, :] = (r.act[pl.ds(n, 1), :] * r.slope[slot, rows, :]).astype(BF16)
        return carry

    lax.fori_loop(0, 32, pre_grad, 0)
    pre_all = r.pre[...].reshape(NT * 256, CHUNK)
    norm_all = r.normed[...].reshape(NT * 256, D)
    for i in range(3):
        cols = slice(i * 128, (i + 1) * 128)
        r.gfull[0, cols, :] = dot_tn(pre_all[:, cols], norm_all) * TEXT_SCALE
    a_high, a_low = split(r.asum[...])
    r.gfull[1] = (dot_tn(a_high, small) + dot_tn(a_low, small)) * TEXT_SCALE

    def pack(k, carry):
        rows = pl.ds(pl.multiple_of(k * OWN, 8), OWN)
        both = jnp.concatenate([r.gfull[0, rows, :], r.gfull[1, rows, :]], axis=0)
        r.gpack[k] = both.astype(BF16)
        return carry

    lax.fori_loop(0, NG, pack, 0)
    r.grecv[g] = r.gpack[g]
    scatter(lambda to: r.gpack.at[to], r.grecv, "gr")

    for step in (1, 2, 3):
        arrived(r.wgy.at[lax.rem(y + 4 - step, 4)], "a2", step)
    quarter = r.wgy[0].astype(F32) + r.wgy[1].astype(F32)
    quarter = quarter + r.wgy[2].astype(F32) + r.wgy[3].astype(F32)
    r.wg2[...] = quarter.astype(BF16)
    r.wgg[g] = r.wg2[g]
    scatter(lambda to: r.wg2.at[to], r.wgg, "a3")

    arrived(r.hid.at[RIM + ROWS :], "rim", 4)
    arrived(r.hid.at[:RIM], "rim", 5)
    for i in range(6):
        rows = slice(i * 256, (i + 1) * 256)
        r.proj2[rows, :] = dot(r.hid[rows, :], r.ns[...]).astype(BF16)
    for i in range(4):
        rows = slice(i * 256, (i + 1) * 256)
        ext = slice(RIM + i * 256, RIM + (i + 1) * 256)
        r.gnn[rows, :] = (dot(r.hid[ext, :], r.ss[...]) + dot(r.e[rows, :], r.proj2[...])).astype(BF16)

    scatter_wait(r.wgg, "a3")
    piece = r.wgg[0].astype(F32)
    for k in range(1, NG):
        piece = piece + r.wgg[k].astype(F32)
    r.wgall[c, y, g] = piece.astype(BF16)
    own_piece = r.wgall.at[c, y, g]

    def piece_out(k, to, source):
        send(own_piece, own_piece, "a4", k, (t, to), start=False).start()

    each_peer(piece_out)

    scatter_wait(r.grecv, "gr")
    summed = r.grecv[0].astype(F32)
    for k in range(1, NG):
        summed = summed + r.grecv[k].astype(F32)
    r.gin[...] = summed[:OWN]
    r.gout[...] = summed[OWN:]

    each_peer(lambda k, to, source: arrived(r.wgall.at[c, y, source], "a4", k))
    own_quarter = r.wgall.at[c, y]
    for step, peer in ((1, up), (2, opp), (3, down)):
        send(own_quarter, own_quarter, "a5", step, (peer, g))
    for step in (1, 2, 3):
        arrived(r.wgall.at[c, lax.rem(y + 4 - step, 4)], "a5", step)
    own_side = r.wgall.at[c]
    send(own_side, own_side, "a6", 0, (sib, g))
    arrived(r.wgall.at[1 - c], "a6", 0)
    for side, first, second in ((0, r.gsf, r.gss), (1, r.gnf, r.gns)):
        for q in range(3):
            first[q * 256 : (q + 1) * 256, :] = r.wgall[side, q].astype(F32).reshape(256, HID)
        second[...] = r.wgall[side, 3].astype(F32).reshape(256, HID)

    for copy in pending:
        copy.wait_send()
    scatter_sent(r.wpack.at[g], "w")
    scatter_sent(own_emb, "eg")
    each_peer(lambda k, to, source: send(own_emb, own_emb, "es", k, (sib, g), start=False).wait_send())
    scatter_sent(r.pick1.at[0], "pg")
    scatter_sent(r.gpack.at[0], "gr")
    scatter_sent(r.wg2.at[0], "a3")
    scatter_sent(own_piece, "a4")


def per_device(states, w_in, w_out, table, adj, sources, node_ids, sf, nf, ss, ns, ups):
    vmem = pl.BlockSpec(memory_space=pltpu.VMEM)
    specs = [vmem] * len(INPUTS)
    specs[INPUTS.index("src")] = pl.BlockSpec(memory_space=pltpu.SMEM)
    scratch = [pltpu.VMEM(shape, dtype) for shape, dtype in SCRATCH.values()]
    for count in SEMS.values():
        scratch += [pltpu.SemaphoreType.DMA((count,)), pltpu.SemaphoreType.DMA((count,))]
    return pl.pallas_call(
        body,
        out_shape=tuple(jax.ShapeDtypeStruct(*spec) for spec in OUTPUTS.values()),
        in_specs=specs,
        out_specs=tuple([vmem] * len(OUTPUTS)),
        scratch_shapes=scratch,
        compiler_params=pltpu.CompilerParams(
            collective_id=0, has_side_effects=True, vmem_limit_bytes=62 * 1024 * 1024
        ),
    )(
        states.reshape(4 * SEQ, D), w_in, w_out, table, adj.reshape(32, 128, 128),
        sources, node_ids.reshape(1, NFT), sf, nf, ss, ns, ups,
    )


def solution(mesh):
    both = ("text", "graph")
    rows = P(both, None)
    return jax.shard_map(
        per_device,
        mesh=mesh,
        in_specs=(
            P(both, None, None), rows, rows, rows, P(both, None, None, None), rows,
            P(), P(), P(), P(), P(), rows,
        ),
        out_specs=(rows, rows, rows, rows, rows, P(), P(), P(), P()),
        check_vma=False,
    )
```

```python
import math
from types import SimpleNamespace

import jax
import jax.numpy as jnp
from jax import lax
from jax.experimental import pallas as pl
from jax.experimental.pallas import tpu as pltpu
from jax.sharding import PartitionSpec as P

MESH = pl.DeviceIdType.MESH
F32 = jnp.float32
BF16 = jnp.bfloat16

D = 768
FFH = 3072
HID = 256
SEQ = 64
ROWS = 1024
RIM = 256
EXT = ROWS + 2 * RIM
NFT = 512
NG = 16
NT = 8
CHUNK = FFH // NT
OWN = FFH // (NT * NG)
NODE_SCALE = 1.0 / math.sqrt(131072)
TEXT_SCALE = 1.0 / math.sqrt(NFT)

INPUTS = {
    "states": ((4 * SEQ, D), BF16),
    "w_in": ((OWN, D), BF16),
    "w_out": ((OWN, D), BF16),
    "ids": ((1, NFT), jnp.int32),
    "src": ((4, 8), jnp.int32),
    "adj": ((32, 128, 128), BF16),
    "ups": ((ROWS, HID), BF16),
    "table": ((ROWS, D), BF16),
    "sf": ((D, HID), BF16),
    "nf": ((D, HID), BF16),
    "ss": ((HID, HID), BF16),
    "ns": ((HID, HID), BF16),
}
HANDED = {
    "gnn": ((ROWS, HID), BF16),
    "fb": ((ROWS, 2 * HID), BF16),
    "early": ((2, 4, 20, 16, 128), BF16),
    "late": ((2, 48, 16, 128), BF16),
    "ngrad": ((4, D), F32),
    "gin": ((OWN, D), F32),
    "gout": ((OWN, D), F32),
}
SCRATCH = {
    "pack_in": ((NG, 2 * OWN, D // 2), BF16),
    "pack_out": ((NG, 2 * OWN, D // 2), BF16),
    "wide": ((CHUNK, D), F32),
    "wi": ((CHUNK, D), BF16),
    "wo": ((CHUNK, D), BF16),
    "normed": ((NT, 256, D), BF16),
    "smean": ((8, D), F32),
    "before": ((256, CHUNK), F32),
    "slope": ((NT, 256, CHUNK), F32),
    "asum": ((32, CHUNK), F32),
    "spread": ((128, CHUNK), F32),
    "turned": ((CHUNK, 128), F32),
    "acols": ((NG, OWN, 128), F32),
    "part": ((32, D), F32),
    "part2": ((2, 16, D), F32),
    "pairin": ((16, D), F32),
    "yemb": ((4, 16, D), BF16),
    "emb": ((2, NG, 16, D), BF16),
    "oh": ((EXT, NFT), BF16),
    "oht": ((NFT, EXT), BF16),
    "keep": ((EXT, 1), F32),
    "e": ((ROWS, EXT), BF16),
    "et": ((EXT, ROWS), BF16),
    "b2": ((EXT, HID), F32),
    "b2out": ((2, RIM, HID), BF16),
    "b2in": ((2, RIM, HID), BF16),
    "back2": ((ROWS, HID), BF16),
    "hg": ((ROWS, HID), F32),
    "tself": ((ROWS, HID), F32),
    "tn": ((EXT, HID), BF16),
    "pn": ((EXT, HID), BF16),
    "embproj": ((NFT, 2 * HID), BF16),
    "hid": ((EXT, HID), BF16),
    "proj2": ((EXT, HID), BF16),
    "b1": ((EXT, HID), F32),
    "b1b": ((EXT, HID), BF16),
    "b1in": ((2, RIM, HID), BF16),
    "feat": ((ROWS, D), BF16),
    "e0": ((2, 80, 16, 128), BF16),
    "e1in": ((80, 16, 128), BF16),
    "e1": ((80, 16, 128), BF16),
    "e2": ((4, 20, 16, 128), BF16),
    "e3out": ((20, 16, 128), BF16),
    "e3": ((NG, 2, 16, 128), BF16),
    "l0": ((2, 48, 16, 128), BF16),
    "l1in": ((48, 16, 128), BF16),
    "l1": ((48, 16, 128), BF16),
    "l2": ((NG, 3, 16, 128), BF16),
    "l3": ((4, 3, 16, 128), BF16),
    "pick": ((2, NG, 16, 2 * HID), BF16),
    "pickin": ((NG, 16, 2 * HID), BF16),
    "pick1": ((NG, 16, 2 * HID), BF16),
    "pickg": ((NG, 16, 2 * HID), BF16),
    "picky": ((4, 16, 2 * HID), BF16),
    "pickall": ((NG, 2, 16, 2 * HID), BF16),
    "nodeg": ((32, D), F32),
    "act": ((32, CHUNK), F32),
    "pre": ((NT, 256, CHUNK), BF16),
    "gfull": ((CHUNK, D), F32),
    "gpack": ((NG, 2 * OWN, D // 2), BF16),
    "grecv": ((NG, 2 * OWN, D // 2), BF16),
}
SEMS = {
    "wi": 16, "wo": 16, "st": 9, "rim": 8, "pair": 1, "ye": 4, "eg": 16, "es": 16,
    "ac": 16, "pk": 1, "pg": 16, "py": 4, "ps": 1, "ag": 16, "as": 16,
    "e1": 1, "e2": 4, "e3": 16, "e4": 16, "e5": 4, "e6": 1,
    "l1": 1, "l2": 16, "l3": 4, "l4": 16, "l5": 1, "gr": 16,
}


def dot(a, b):
    return jnp.dot(a, b, preferred_element_type=F32)


def dot_nt(a, b):
    return lax.dot_general(a, b, (((1,), (1,)), ((), ())), preferred_element_type=F32)


def dot_tn(a, b):
    return lax.dot_general(a, b, (((0,), (0,)), ((), ())), preferred_element_type=F32)


def gelu_pair(v):
    cdf = 0.5 * (1.0 + lax.erf(v * (1.0 / math.sqrt(2.0))))
    return v * cdf, cdf + v * jnp.exp(-0.5 * v * v) * (1.0 / math.sqrt(2.0 * math.pi))


def split(v):
    high = v.astype(BF16)
    return high, (v - high.astype(F32)).astype(BF16)


def body(*refs):
    taken = iter(refs)
    given = {name: next(taken) for name in INPUTS}
    handed = {name: next(taken) for name in HANDED}
    r = SimpleNamespace()
    for name in (*INPUTS, *HANDED, *SCRATCH):
        setattr(r, name, next(taken))
    sems = {name: (next(taken), next(taken)) for name in SEMS}
    fetch_sems, hand_sems = next(taken), next(taken)
    fetches = {
        name: pltpu.make_async_copy(given[name], getattr(r, name), fetch_sems.at[k])
        for k, name in enumerate(INPUTS)
    }
    for copy in fetches.values():
        copy.start()
    handing = []

    def fetched(*wanted):
        for name in wanted:
            fetches[name].wait()

    def hand(name):
        at = list(HANDED).index(name)
        copy = pltpu.make_async_copy(getattr(r, name), handed[name], hand_sems.at[at])
        copy.start()
        handing.append(copy)

    t = lax.axis_index("text")
    g = lax.axis_index("graph")
    c = lax.rem(t, 2)
    y = lax.div(t, 2)
    sib = t + 1 - 2 * c

    def at_y(step):
        return lax.rem(y + step, 4) * 2 + c

    up, opp, down = at_y(1), at_y(2), at_y(3)
    x, z = lax.div(g, 4), lax.rem(g, 4)

    def at_x(step):
        return lax.rem(x + step, 4)

    def at_z(step):
        return lax.rem(z + step, 4)

    ahead = lax.rem(g + 1, NG)
    behind = lax.rem(g + NG - 1, NG)
    pending = []

    def send(src, dst, kind, tag, to, start=True):
        copy = pltpu.make_async_remote_copy(
            src_ref=src, dst_ref=dst, send_sem=sems[kind][0].at[tag],
            recv_sem=sems[kind][1].at[tag], device_id=to, device_id_type=MESH,
        )
        if start:
            copy.start()
            pending.append(copy)
        return copy

    def arrived(dst, kind, tag):
        send(dst, dst, kind, tag, (sib, g), start=False).wait_recv()

    def each_peer(fn):
        def step(k, carry):
            fn(k, lax.rem(g + k, NG), lax.rem(g + NG - k, NG))
            return carry

        lax.fori_loop(1, NG, step, 0)

    def scatter(src_of, dst, kind):
        def one(k, to, source):
            pltpu.make_async_remote_copy(
                src_ref=src_of(to), dst_ref=dst.at[g], send_sem=sems[kind][0].at[k],
                recv_sem=sems[kind][1].at[k], device_id=(t, to), device_id_type=MESH,
            ).start()

        each_peer(one)

    def scatter_wait(dst, kind):
        each_peer(lambda k, to, source: arrived(dst.at[source], kind, k))

    def scatter_sent(src, kind):
        def one(k, to, source):
            send(src, src, kind, k, (t, to), start=False).wait_send()

        each_peer(one)

    barrier = pltpu.get_barrier_semaphore()

    def greet(to):
        pl.semaphore_signal(barrier, inc=1, device_id=to, device_id_type=MESH)

    for peer in (sib, up, opp, down):
        greet((peer, g))
    each_peer(lambda k, to, source: greet((t, to)))

    fetched("w_in", "w_out", "states")

    def halves(rows):
        return jnp.concatenate([rows[:, : D // 2], rows[:, D // 2 :]], axis=0)

    def joined(rows):
        return jnp.concatenate([rows[:OWN], rows[OWN:]], axis=1)

    r.pack_in[g] = halves(r.w_in[...].astype(F32)).astype(BF16)
    r.pack_out[z * 4 + x] = halves(r.w_out[...].astype(F32)).astype(BF16)

    for i in range(4):
        own = r.states[i * SEQ : (i + 1) * SEQ, :].astype(F32)
        r.smean[i : i + 1, :] = jnp.sum(own, axis=0, keepdims=True) * (1.0 / SEQ)
        mean = jnp.mean(own, axis=1, keepdims=True)
        centered = own - mean
        var = jnp.mean(centered * centered, axis=1, keepdims=True)
        r.normed[t, i * SEQ : (i + 1) * SEQ, :] = (centered * lax.rsqrt(var + 1e-05)).astype(BF16)
    fetched("table", "sf", "nf")
    for i in range(4):
        rows = slice(i * 256, (i + 1) * 256)
        nodes = r.table[rows, :]
        r.tn[RIM + i * 256 : RIM + (i + 1) * 256, :] = dot(nodes, r.nf[...]).astype(BF16)
        r.tself[rows, :] = dot(nodes, r.sf[...])

    pl.semaphore_wait(barrier, 19)
    own_in, own_out = r.pack_in.at[g], r.pack_out.at[z * 4 + x]
    for step in (1, 3, 2):
        send(own_in, own_in, "wi", step, (t, x * 4 + at_z(step)))
        send(own_out, own_out, "wo", step, (t, at_x(step) * 4 + z))
    mine = r.normed.at[t]
    send(mine, mine, "st", 0, (sib, g))
    send(mine, mine, "st", 1, (up, g))
    send(mine, mine, "st", 2, (down, g))

    fetched("adj", "src")
    def tiles(b, carry):
        rows = pl.ds(pl.multiple_of(b * 128, 128), 128)
        plain = [r.adj[b * 4 + k] for k in range(4)]
        turned = [p.astype(F32).T.astype(BF16) for p in plain]
        here = lax.broadcasted_iota(jnp.int32, (4, 8), 1) == b
        source = jnp.sum(jnp.where(here, r.src[...].astype(F32), 0.0), axis=1, keepdims=True)
        for s in range(12):
            hits = jnp.where(source == float(s), 1.0, 0.0)
            own = jnp.zeros((128, 128), BF16)
            other = jnp.zeros((128, 128), BF16)
            for k in range(4):
                hit = jnp.broadcast_to(hits[k : k + 1, :], (128, 128)).astype(BF16)
                own = own + plain[k] * hit
                other = other + turned[k] * hit
            r.e[rows, s * 128 : (s + 1) * 128] = own
            r.et[s * 128 : (s + 1) * 128, rows] = other
        return carry

    lax.fori_loop(0, 8, tiles, 0)

    for step in (1, 2, 3):
        arrived(r.pack_in.at[x * 4 + at_z(4 - step)], "wi", step)
    slab = r.pack_in.at[pl.ds(x * 4, 4)]
    for step in (1, 3, 2):
        send(slab, slab, "wi", 4 + step, (t, at_x(step) * 4 + z))
    for step in (1, 2, 3):
        arrived(r.pack_out.at[z * 4 + at_x(4 - step)], "wo", step)
    slab = r.pack_out.at[pl.ds(z * 4, 4)]
    for step in (1, 3, 2):
        send(slab, slab, "wo", 4 + step, (t, x * 4 + at_z(step)))

    fetched("ups", "ss", "ns")
    for i in (0, 5, 1, 2, 3, 4):
        rows = slice(i * 256, (i + 1) * 256)
        r.b2[rows, :] = dot(r.et[rows, :], r.ups[...])

    fetched("ids")
    row = lax.broadcasted_iota(jnp.int32, (NFT, NFT), 0)
    col = lax.broadcasted_iota(jnp.int32, (NFT, NFT), 1)
    wanted = (col & 256) + ((col >> 2) & 3) * 64 + ((col >> 4) & 15) * 4 + (col & 3)
    moved = jnp.where(row == wanted, 1.0, 0.0).astype(BF16)
    ids = jnp.broadcast_to(r.ids[...], (8, NFT))
    pieces = [((ids >> shift) & 63).astype(F32).astype(BF16) for shift in (0, 6, 12)]
    low, middle, high = [dot(p, moved) for p in pieces]
    spot = low + 64.0 * middle + 4096.0 * high
    spot_row = spot[:1, :]
    spot_col = jnp.broadcast_to(spot_row, (128, NFT)).T
    device = t * NG + g
    starts = [(t * NG + behind) * ROWS + 768 + e * 128 for e in range(2)]
    starts += [device * ROWS + e * 128 for e in range(8)]
    starts += [(t * NG + ahead) * ROWS + e * 128 for e in range(2)]
    for e in range(12):
        start = starts[e].astype(F32)
        down_rows = lax.broadcasted_iota(jnp.int32, (128, NFT), 0).astype(F32) + start
        hit = jnp.where(down_rows == spot_row, 1.0, 0.0)
        r.oh[e * 128 : (e + 1) * 128, :] = hit.astype(BF16)
        r.keep[e * 128 : (e + 1) * 128, :] = 1.0 - jnp.sum(hit, axis=1, keepdims=True)
        across = lax.broadcasted_iota(jnp.int32, (NFT, 128), 1).astype(F32) + start
        r.oht[:, e * 128 : (e + 1) * 128] = jnp.where(across == spot_col, 1.0, 0.0).astype(BF16)

    def unpack(packed, out, place):
        def step(k, carry):
            rows = pl.ds(pl.multiple_of(k * OWN, 8), OWN)
            r.wide[rows, :] = joined(packed[place(k)].astype(F32))
            return carry

        lax.fori_loop(0, NG, step, 0)
        out[...] = r.wide[...].astype(BF16)

    for step in (1, 2, 3):
        arrived(r.pack_in.at[pl.ds(at_x(4 - step) * 4, 4)], "wi", 4 + step)
    unpack(r.pack_in, r.wi, lambda k: k)

    def encode(slot):
        r.before[...] = dot_nt(r.normed[slot], r.wi[...])

        def node(i, carry):
            rows = pl.ds(pl.multiple_of(i * SEQ, SEQ), SEQ)
            value, slope = gelu_pair(r.before[rows, :])
            r.slope[slot, rows, :] = slope
            r.asum[pl.ds(slot * 4 + i, 1), :] = jnp.sum(value, axis=0, keepdims=True)
            return carry

        lax.fori_loop(0, 4, node, 0)

    def fellow(slot):
        return slot + 1 - 2 * c

    encode(t)
    from_down, from_up, far = r.normed.at[down], r.normed.at[up], r.normed.at[opp]
    arrived(from_down, "st", 1)
    send(from_down.at[:128], from_down.at[:128], "st", 3, (up, g))
    send(from_down, from_down, "st", 5, (sib, g))
    arrived(from_up, "st", 2)
    send(from_up.at[128:], from_up.at[128:], "st", 4, (down, g))
    send(from_up, from_up, "st", 6, (sib, g))
    arrived(r.normed.at[sib], "st", 0)
    encode(sib)
    send(r.tn.at[RIM : 2 * RIM], r.tn.at[RIM + ROWS :], "rim", 0, (t, behind))
    send(r.tn.at[ROWS : ROWS + RIM], r.tn.at[:RIM], "rim", 1, (t, ahead))
    r.b2out[0] = r.b2[:RIM, :].astype(BF16)
    r.b2out[1] = r.b2[RIM + ROWS :, :].astype(BF16)
    send(r.b2out.at[0], r.b2in.at[1], "rim", 2, (t, behind))
    send(r.b2out.at[1], r.b2in.at[0], "rim", 3, (t, ahead))
    encode(down)
    encode(up)
    arrived(far.at[:128], "st", 3)
    send(far.at[:128], far.at[:128], "st", 7, (sib, g))
    arrived(far.at[128:], "st", 4)
    send(far.at[128:], far.at[128:], "st", 8, (sib, g))
    arrived(r.normed.at[fellow(down)], "st", 5)
    encode(fellow(down))
    arrived(r.normed.at[fellow(up)], "st", 6)
    encode(fellow(up))
    encode(opp)
    far_pair = r.normed.at[fellow(opp)]
    arrived(far_pair.at[:128], "st", 7)
    arrived(far_pair.at[128:], "st", 8)
    encode(fellow(opp))

    for step in (1, 2, 3):
        arrived(r.pack_out.at[pl.ds(at_z(4 - step) * 4, 4)], "wo", 4 + step)
    unpack(r.pack_out, r.wo, lambda k: (k % 4) * 4 + k // 4)
    a_high, a_low = split(r.asum[...] * (1.0 / SEQ))
    r.part[...] = dot(a_high, r.wo[...]) + dot(a_low, r.wo[...])
    for i in range(4):
        spot_rows = pl.ds(t * 4 + i, 1)
        r.part[spot_rows, :] = r.part[spot_rows, :] + r.smean[i : i + 1, :]
    r.part2[0] = r.part[:16, :]
    r.part2[1] = r.part[16:, :]
    send(r.part2.at[1 - c], r.pairin, "pair", 0, (sib, g))
    arrived(r.pairin, "pair", 0)
    r.yemb[y] = (r.part2[c] + r.pairin[...]).astype(BF16)
    for step, peer in ((1, up), (2, opp), (3, down)):
        send(r.yemb.at[y], r.yemb.at[y], "ye", step, (peer, g))
    for step in (1, 2, 3):
        arrived(r.yemb.at[lax.rem(y + 4 - step, 4)], "ye", step)
    total = r.yemb[0].astype(F32) + r.yemb[1].astype(F32)
    total = total + r.yemb[2].astype(F32) + r.yemb[3].astype(F32)
    r.emb[c, g] = total.astype(BF16)

    def emb_out(k, to, source):
        ref = r.emb.at[c, g]
        send(ref, ref, "eg", k, (t, to), start=False).start()

    each_peer(emb_out)
    own_emb = r.emb.at[c, g]
    send(own_emb, own_emb, "es", 0, (sib, g))

    r.spread[...] = jnp.zeros_like(r.spread)
    r.spread[pl.ds(pl.multiple_of(lax.rem(g, 4) * 32, 32), 32), :] = r.asum[...]
    r.turned[...] = r.spread[...].T
    my_units = pl.ds(pl.multiple_of(g * OWN, 8), OWN)
    r.acols[g] = r.turned[my_units, :]

    arrived(r.b2in.at[0], "rim", 3)
    arrived(r.b2in.at[1], "rim", 2)
    r.b2[RIM : 2 * RIM, :] = r.b2[RIM : 2 * RIM, :] + r.b2in[0].astype(F32)
    r.b2[ROWS : ROWS + RIM, :] = r.b2[ROWS : ROWS + RIM, :] + r.b2in[1].astype(F32)
    r.back2[...] = r.b2[RIM : RIM + ROWS, :].astype(BF16)
    for i in range(4):
        rows = slice(i * 256, (i + 1) * 256)
        r.hg[rows, :] = dot_nt(r.ups[rows, :], r.ss[...]) + dot_nt(r.back2[rows, :], r.ns[...])
    arrived(r.tn.at[RIM + ROWS :], "rim", 0)
    arrived(r.tn.at[:RIM], "rim", 1)

    def emb_on(k, to, source):
        ref = r.emb.at[c, source]
        arrived(ref, "eg", k)
        send(ref, ref, "es", k, (sib, g), start=False).start()

    each_peer(emb_on)
    arrived(r.emb.at[1 - c, g], "es", 0)
    each_peer(lambda k, to, source: arrived(r.emb.at[1 - c, source], "es", k))

    scatter(lambda to: r.turned.at[pl.ds(pl.multiple_of(to * OWN, 8), OWN)], r.acols, "ac")

    emb_all = r.emb[...].reshape(NFT, D)
    r.embproj[:, :HID] = dot(emb_all, r.sf[...]).astype(BF16)
    r.embproj[:, HID:] = dot(emb_all, r.nf[...]).astype(BF16)
    for i in range(6):
        rows = slice(i * 256, (i + 1) * 256)
        new = dot(r.oh[rows, :], r.embproj[:, HID:])
        r.pn[rows, :] = (r.tn[rows, :].astype(F32) * r.keep[rows, :] + new).astype(BF16)

    for i in range(4):
        rows = slice(i * 256, (i + 1) * 256)
        ext = slice(RIM + i * 256, RIM + (i + 1) * 256)
        pre = r.tself[rows, :] * r.keep[ext, :] + dot(r.oh[ext, :], r.embproj[:, :HID])
        pre = pre + dot(r.e[rows, :], r.pn[...])
        value, slope = gelu_pair(pre)
        r.hid[ext, :] = value.astype(BF16)
        r.fb[rows, :HID] = (r.hg[rows, :] * slope).astype(BF16)
    for i in (0, 5, 1, 2, 3, 4):
        rows = slice(i * 256, (i + 1) * 256)
        term = dot(r.et[rows, :], r.fb[:, :HID])
        r.b1[rows, :] = term
        r.b1b[rows, :] = term.astype(BF16)
    send(r.b1b.at[:RIM], r.b1in.at[1], "rim", 6, (t, behind))
    send(r.b1b.at[RIM + ROWS :], r.b1in.at[0], "rim", 7, (t, ahead))

    for i in range(2):
        rows = slice(i * 256, (i + 1) * 256)
        first = dot(r.oht[rows, RIM : RIM + ROWS], r.fb[:, :HID]).astype(BF16)
        back = dot(r.oht[rows, :], r.b1b[...]).astype(BF16)
        r.pick[i, :, :, :HID] = first.reshape(NG, 16, HID)
        r.pick[i, :, :, HID:] = back.reshape(NG, 16, HID)
    send(r.pick.at[1 - c], r.pickin, "pk", 0, (sib, g))

    def features(i):
        rows = slice(i * 256, (i + 1) * 256)
        ext = slice(RIM + i * 256, RIM + (i + 1) * 256)
        old = r.table[rows, :].astype(F32) * r.keep[ext, :]
        r.feat[rows, :] = (old + dot(r.oh[ext, :], emb_all)).astype(BF16)

    for i in range(4):
        features(i)
    arrived(r.pickin, "pk", 0)
    r.pick1[...] = (r.pick[c].astype(F32) + r.pickin[...].astype(F32)).astype(BF16)
    r.pickg[g] = r.pick1[g]
    scatter(lambda to: r.pick1.at[to], r.pickg, "pg")

    def keep_grad(buffer, first, left, right):
        for q in range(left.shape[1] // 256):
            term = dot_tn(left[:, q * 256 : (q + 1) * 256], right) * NODE_SCALE
            at = slice(first + q * 16, first + q * 16 + 16)
            for side in range(2):
                cols = slice(side * 128, (side + 1) * 128)
                buffer[side, at] = term[:, cols].astype(BF16).reshape(16, 16, 128)

    hidden = r.hid[RIM : RIM + ROWS, :]
    keep_grad(r.e0, 48, hidden, r.ups[...])
    keep_grad(r.e0, 64, hidden, r.back2[...])
    keep_grad(r.e0, 0, r.feat, r.fb[:, :HID])
    send(r.e0.at[1 - c], r.e1in, "e1", 0, (sib, g))

    arrived(r.b1in.at[0], "rim", 7)
    arrived(r.b1in.at[1], "rim", 6)
    r.b1[RIM : 2 * RIM, :] = r.b1[RIM : 2 * RIM, :] + r.b1in[0].astype(F32)
    r.b1[ROWS : ROWS + RIM, :] = r.b1[ROWS : ROWS + RIM, :] + r.b1in[1].astype(F32)
    r.fb[:, HID:] = r.b1[RIM : RIM + ROWS, :].astype(BF16)
    hand("fb")
    arrived(r.e1in, "e1", 0)
    r.e1[...] = (r.e0[c].astype(F32) + r.e1in[...].astype(F32)).astype(BF16)
    r.e2[y] = r.e1[pl.ds(y * 20, 20)]
    for step in (1, 3, 2):
        to_y = lax.rem(y + step, 4)
        send(r.e1.at[pl.ds(to_y * 20, 20)], r.e2.at[y], "e2", step, (to_y * 2 + c, g))
    keep_grad(r.l0, 0, r.feat, r.fb[:, HID:])
    send(r.l0.at[1 - c], r.l1in, "l1", 0, (sib, g))

    def over_peers(ref):
        total = ref[0].astype(F32)
        for k in range(1, NG):
            total = total + ref[k].astype(F32)
        return total

    def over_y(ref):
        return (ref[0].astype(F32) + ref[1].astype(F32)) + (ref[2].astype(F32) + ref[3].astype(F32))

    scatter_wait(r.pickg, "pg")
    r.picky[y] = over_peers(r.pickg).astype(BF16)
    for step, peer in ((1, up), (2, opp), (3, down)):
        send(r.picky.at[y], r.picky.at[y], "py", step, (peer, g))
    arrived(r.l1in, "l1", 0)
    r.l1[...] = (r.l0[c].astype(F32) + r.l1in[...].astype(F32)).astype(BF16)
    r.l2[g] = r.l1[pl.ds(g * 3, 3)]
    scatter(lambda to: r.l1.at[pl.ds(to * 3, 3)], r.l2, "l2")
    for step in (1, 2, 3):
        arrived(r.picky.at[lax.rem(y + 4 - step, 4)], "py", step)
    r.pickall[g, c] = over_y(r.picky).astype(BF16)
    own_picks = r.pickall.at[g, c]
    send(own_picks, own_picks, "ps", 0, (sib, g))

    def picks_out(k, to, source):
        send(own_picks, own_picks, "ag", k, (t, to), start=False).start()

    each_peer(picks_out)
    send(r.hid.at[RIM : 2 * RIM], r.hid.at[RIM + ROWS :], "rim", 4, (t, behind))
    send(r.hid.at[ROWS : ROWS + RIM], r.hid.at[:RIM], "rim", 5, (t, ahead))

    arrived(r.pickall.at[g, 1 - c], "ps", 0)
    rows32 = r.pickall[g].reshape(32, 2 * HID)

    def node_grads(rows):
        return dot_nt(rows[:, :HID], r.sf[...]) + dot_nt(rows[:, HID:], r.nf[...])

    node_grad = node_grads(rows32)
    r.nodeg[...] = node_grad
    for i in range(4):
        r.ngrad[i : i + 1, :] = r.nodeg[pl.ds(t * 4 + i, 1), :]
    hand("ngrad")
    small = (node_grad * (1.0 / SEQ)).astype(BF16)
    r.act[...] = dot_nt(small, r.wo[...])

    def pre_grad(n, carry):
        slot = n // 4
        rows = pl.ds(pl.multiple_of((n % 4) * SEQ, SEQ), SEQ)
        r.pre[slot, rows, :] = (r.act[pl.ds(n, 1), :] * r.slope[slot, rows, :]).astype(BF16)
        return carry

    lax.fori_loop(0, 32, pre_grad, 0)
    pre_all = r.pre[...].reshape(NT * 256, CHUNK)
    norm_all = r.normed[...].reshape(NT * 256, D)
    for i in range(3):
        cols = slice(i * 128, (i + 1) * 128)
        r.gfull[cols, :] = dot_tn(pre_all[:, cols], norm_all) * TEXT_SCALE

    def pack(k, carry):
        rows = pl.ds(pl.multiple_of(k * OWN, 8), OWN)
        r.gpack[k] = halves(r.gfull[rows, :]).astype(BF16)
        return carry

    lax.fori_loop(0, NG, pack, 0)
    r.grecv[g] = r.gpack[g]
    scatter(lambda to: r.gpack.at[to], r.grecv, "gr")

    scatter_wait(r.l2, "l2")
    r.l3[y] = over_peers(r.l2).astype(BF16)
    for step, peer in ((1, up), (2, opp), (3, down)):
        send(r.l3.at[y], r.l3.at[y], "l3", step, (peer, g))
    for step in (1, 2, 3):
        arrived(r.e2.at[lax.rem(y + 4 - step, 4)], "e2", step)
    r.e3out[...] = over_y(r.e2).astype(BF16)

    def piece_out(k, to, source):
        @pl.when(to < 10)
        def _():
            send(r.e3out.at[pl.ds(to * 2, 2)], r.e3.at[g], "e3", k, (t, to), start=False).start()

    each_peer(piece_out)

    def picks_on(k, to, source):
        ref = r.pickall.at[source, c]
        arrived(ref, "ag", k)
        send(ref, ref, "as", k, (sib, g), start=False).start()

    each_peer(picks_on)

    for step in (1, 2, 3):
        arrived(r.l3.at[lax.rem(y + 4 - step, 4)], "l3", step)
    r.late[c, pl.ds(g * 3, 3)] = over_y(r.l3).astype(BF16)
    own_late = r.late.at[c, pl.ds(g * 3, 3)]

    def late_out(k, to, source):
        send(own_late, own_late, "l4", k, (t, to), start=False).start()

    each_peer(late_out)

    @pl.when(g < 10)
    def _():
        r.e3[g] = r.e3out[pl.ds(g * 2, 2)]
        scatter_wait(r.e3, "e3")
        r.early[c, y, pl.ds(g * 2, 2)] = over_peers(r.e3).astype(BF16)
        own = r.early.at[c, y, pl.ds(g * 2, 2)]

        def early_out(k, to, source):
            send(own, own, "e4", k, (t, to), start=False).start()

        each_peer(early_out)

    arrived(r.hid.at[RIM + ROWS :], "rim", 4)
    arrived(r.hid.at[:RIM], "rim", 5)
    for i in range(6):
        rows = slice(i * 256, (i + 1) * 256)
        r.proj2[rows, :] = dot(r.hid[rows, :], r.ns[...]).astype(BF16)
    for i in range(4):
        rows = slice(i * 256, (i + 1) * 256)
        ext = slice(RIM + i * 256, RIM + (i + 1) * 256)
        r.gnn[rows, :] = (dot(r.hid[ext, :], r.ss[...]) + dot(r.e[rows, :], r.proj2[...])).astype(BF16)
    hand("gnn")

    each_peer(lambda k, to, source: arrived(r.late.at[c, pl.ds(source * 3, 3)], "l4", k))
    send(r.late.at[c], r.late.at[c], "l5", 0, (sib, g))

    def early_in(k, to, source):
        @pl.when(source < 10)
        def _():
            arrived(r.early.at[c, y, pl.ds(source * 2, 2)], "e4", k)

    each_peer(early_in)
    own_quarter = r.early.at[c, y]
    for step, peer in ((1, up), (3, down), (2, opp)):
        send(own_quarter, own_quarter, "e5", step, (peer, g))

    scatter_wait(r.acols, "ac")
    each_peer(lambda k, to, source: arrived(r.pickall.at[source, 1 - c], "as", k))
    small_all = (node_grads(r.pickall[...].reshape(NFT, 2 * HID)) * (1.0 / SEQ)).astype(BF16)
    units = jnp.zeros((OWN, D), F32)
    for q in range(4):
        lanes = (r.acols[4 * q] + r.acols[4 * q + 1]) + (r.acols[4 * q + 2] + r.acols[4 * q + 3])
        a_high, a_low = split(lanes)
        block = small_all[q * 128 : (q + 1) * 128]
        units = units + (dot(a_high, block) + dot(a_low, block))
    r.gout[...] = units * TEXT_SCALE
    hand("gout")

    scatter_wait(r.grecv, "gr")
    r.gin[...] = joined(over_peers(r.grecv))
    hand("gin")

    arrived(r.late.at[1 - c], "l5", 0)
    hand("late")
    for step in (1, 2, 3):
        arrived(r.early.at[c, lax.rem(y + 4 - step, 4)], "e5", step)
    send(r.early.at[c], r.early.at[c], "e6", 0, (sib, g))
    arrived(r.early.at[1 - c], "e6", 0)
    hand("early")

    for copy in pending:
        copy.wait_send()
    scatter_sent(own_emb, "eg")
    each_peer(lambda k, to, source: send(own_emb, own_emb, "es", k, (sib, g), start=False).wait_send())
    scatter_sent(r.acols.at[0], "ac")
    scatter_sent(r.pick1.at[0], "pg")
    scatter_sent(own_picks, "ag")
    each_peer(lambda k, to, source: send(own_picks, own_picks, "as", k, (sib, g), start=False).wait_send())
    scatter_sent(r.gpack.at[0], "gr")
    scatter_sent(r.l2.at[0], "l2")
    scatter_sent(own_late, "l4")

    def piece_sent(k, to, source):
        @pl.when(to < 10)
        def _():
            send(r.e3.at[0], r.e3.at[0], "e3", k, (t, to), start=False).wait_send()

    each_peer(piece_sent)

    @pl.when(g < 10)
    def _():
        scatter_sent(r.e3.at[0], "e4")

    for copy in handing:
        copy.wait()


def finish(fb, gnn, early, late, ngrad, gin, gout, sf, nf, gnn_o, tgrad, ngrad_o, gin_o, gout_o, gsf, gnf, gss, gns):
    tgrad[...] = dot_nt(fb[:, :HID], sf[...]) + dot_nt(fb[:, HID:], nf[...])
    gnn_o[...] = gnn[...]

    @pl.when(pl.program_id(0) == 0)
    def _():
        ngrad_o[...] = ngrad[...]
        gin_o[...] = gin[...]
        gout_o[...] = gout[...]
        for c in range(2):
            cols = slice(c * 128, (c + 1) * 128)
            gsf[:, cols] = early[c, :48].astype(F32).reshape(D, 128)
            gss[:, cols] = early[c, 48:64].astype(F32).reshape(HID, 128)
            gns[:, cols] = early[c, 64:].astype(F32).reshape(HID, 128)
            gnf[:, cols] = late[c].astype(F32).reshape(D, 128)


def per_device(states, w_in, w_out, table, adj, sources, node_ids, sf, nf, ss, ns, ups):
    anywhere = pl.BlockSpec(memory_space=pl.ANY)
    scratch = []
    for kind in (INPUTS, HANDED, SCRATCH):
        scratch += [pltpu.VMEM(shape, dtype) for shape, dtype in kind.values()]
    for count in SEMS.values():
        scratch += [pltpu.SemaphoreType.DMA((count,)), pltpu.SemaphoreType.DMA((count,))]
    scratch += [pltpu.SemaphoreType.DMA((len(INPUTS),)), pltpu.SemaphoreType.DMA((len(HANDED),))]
    gnn, fb, early, late, ngrad, gin, gout = pl.pallas_call(
        body,
        out_shape=tuple(jax.ShapeDtypeStruct(*spec) for spec in HANDED.values()),
        in_specs=[anywhere] * len(INPUTS),
        out_specs=tuple([anywhere] * len(HANDED)),
        scratch_shapes=scratch,
        compiler_params=pltpu.CompilerParams(
            collective_id=0, has_side_effects=True, vmem_limit_bytes=62 * 1024 * 1024
        ),
    )(
        states.reshape(4 * SEQ, D), w_in, w_out, node_ids.reshape(1, NFT), sources.T,
        adj.reshape(32, 128, 128), ups, table, sf, nf, ss, ns,
    )

    def whole(*shape):
        return pl.BlockSpec(shape, lambda i: (0,) * len(shape))

    def block(wide):
        return pl.BlockSpec((256, wide), lambda i: (i, 0))

    small = [whole(4, D), whole(OWN, D), whole(OWN, D)]
    square = whole(HID, HID)
    shapes = [
        ((ROWS, HID), BF16), ((ROWS, D), F32), ((4, D), F32), ((OWN, D), F32), ((OWN, D), F32),
        ((D, HID), F32), ((D, HID), F32), ((HID, HID), F32), ((HID, HID), F32),
    ]
    return tuple(pl.pallas_call(
        finish,
        grid=(4,),
        out_shape=[jax.ShapeDtypeStruct(*shape) for shape in shapes],
        in_specs=[
            block(2 * HID), block(HID), whole(2, 80, 16, 128), whole(2, 48, 16, 128), *small,
            whole(D, HID), whole(D, HID),
        ],
        out_specs=[block(HID), block(D), *small, whole(D, HID), whole(D, HID), square, square],
        compiler_params=pltpu.CompilerParams(vmem_limit_bytes=62 * 1024 * 1024),
    )(fb, gnn, early.reshape(2, 80, 16, 128), late, ngrad, gin, gout, sf, nf))


def solution(mesh):
    both = ("text", "graph")
    rows = P(both, None)
    return jax.shard_map(
        per_device,
        mesh=mesh,
        in_specs=(
            P(both, None, None), rows, rows, rows, P(both, None, None, None), rows,
            P(), P(), P(), P(), P(), rows,
        ),
        out_specs=(rows, rows, rows, rows, rows, P(), P(), P(), P()),
        check_vma=False,
    )
```

```python
import math
from types import SimpleNamespace

import jax
import jax.numpy as jnp
from jax import lax
from jax.experimental import pallas as pl
from jax.experimental.pallas import tpu as pltpu
from jax.sharding import PartitionSpec as P

MESH = pl.DeviceIdType.MESH
F32 = jnp.float32
BF16 = jnp.bfloat16

D = 768
FFH = 3072
HID = 256
SEQ = 64
ROWS = 1024
RIM = 256
EXT = ROWS + 2 * RIM
NFT = 512
NG = 16
NT = 8
CHUNK = FFH // NT
OWN = FFH // (NT * NG)
NODE_SCALE = 1.0 / math.sqrt(131072)
TEXT_SCALE = 1.0 / math.sqrt(NFT)

INPUTS = {
    "states": ((4 * SEQ, D), BF16),
    "w_in": ((OWN, D), BF16),
    "w_out": ((OWN, D), BF16),
    "ids": ((1, NFT), jnp.int32),
    "src": ((4, 8), jnp.int32),
    "adj": ((32, 128, 128), BF16),
    "ups": ((ROWS, HID), BF16),
    "table": ((ROWS, D), BF16),
    "sf": ((D, HID), BF16),
    "nf": ((D, HID), BF16),
    "ss": ((HID, HID), BF16),
    "ns": ((HID, HID), BF16),
}
HANDED = {
    "gnn": ((ROWS, HID), BF16),
    "fb": ((ROWS, 2 * HID), BF16),
    "early": ((2, 4, 20, 16, 128), BF16),
    "late": ((2, 48, 16, 128), BF16),
    "ngrad": ((4, D), F32),
    "gin": ((OWN, D), F32),
    "gout": ((OWN, D), F32),
}
SCRATCH = {
    "pack_in": ((NG, 2 * OWN, D // 2), BF16),
    "pack_out": ((NG, 2 * OWN, D // 2), BF16),
    "wide": ((CHUNK, D), F32),
    "wi": ((CHUNK, D), BF16),
    "wo": ((CHUNK, D), BF16),
    "normed": ((NT, 256, D), BF16),
    "smean": ((8, D), F32),
    "before": ((256, CHUNK), F32),
    "slope": ((NT, 256, CHUNK), F32),
    "asum": ((32, CHUNK), F32),
    "spread": ((128, CHUNK), F32),
    "turned": ((CHUNK, 128), F32),
    "acols": ((NG, OWN, 128), F32),
    "part": ((32, D), F32),
    "part2": ((2, 16, D), F32),
    "pairin": ((16, D), F32),
    "yemb": ((4, 16, D), BF16),
    "emb": ((2, NG, 16, D), BF16),
    "oh": ((EXT, NFT), BF16),
    "oht": ((NFT, EXT), BF16),
    "keep": ((EXT, 1), F32),
    "e": ((ROWS, EXT), BF16),
    "et": ((EXT, ROWS), BF16),
    "b2": ((EXT, HID), F32),
    "b2out": ((2, RIM, HID), BF16),
    "b2in": ((2, RIM, HID), BF16),
    "back2": ((ROWS, HID), BF16),
    "hg": ((ROWS, HID), F32),
    "tself": ((ROWS, HID), F32),
    "tn": ((EXT, HID), BF16),
    "pn": ((EXT, HID), BF16),
    "embproj": ((NFT, 2 * HID), BF16),
    "hid": ((EXT, HID), BF16),
    "proj2": ((EXT, HID), BF16),
    "b1": ((EXT, HID), F32),
    "b1b": ((EXT, HID), BF16),
    "b1in": ((2, RIM, HID), BF16),
    "feat": ((ROWS, D), BF16),
    "e0": ((2, 80, 16, 128), BF16),
    "e1in": ((80, 16, 128), BF16),
    "e1": ((80, 16, 128), BF16),
    "e2": ((4, 20, 16, 128), BF16),
    "e3out": ((20, 16, 128), BF16),
    "e3": ((NG, 2, 16, 128), BF16),
    "l0": ((2, 48, 16, 128), BF16),
    "l1in": ((48, 16, 128), BF16),
    "l1": ((48, 16, 128), BF16),
    "l2": ((NG, 3, 16, 128), BF16),
    "l3": ((4, 3, 16, 128), BF16),
    "pick": ((2, NG, 16, 2 * HID), BF16),
    "pickin": ((NG, 16, 2 * HID), BF16),
    "pick1": ((NG, 16, 2 * HID), BF16),
    "pickg": ((NG, 16, 2 * HID), BF16),
    "picky": ((4, 16, 2 * HID), BF16),
    "pickall": ((NG, 2, 16, 2 * HID), BF16),
    "nodeg": ((32, D), F32),
    "act": ((32, CHUNK), F32),
    "pre": ((NT, 256, CHUNK), BF16),
    "gfull": ((CHUNK, D), F32),
    "gpack": ((NG, 2 * OWN, D // 2), BF16),
    "grecv": ((NG, 2 * OWN, D // 2), BF16),
}
SEMS = {
    "wi": 16, "wo": 16, "st": 11, "rim": 8, "pair": 1, "ye": 4, "eg": 16, "es": 16,
    "ac": 16, "pk": 1, "pg": 16, "py": 4, "ps": 1, "ag": 16, "as": 16,
    "e1": 1, "e2": 4, "e3": 16, "e4": 16, "e5": 4, "e6": 1,
    "l1": 1, "l2": 16, "l3": 4, "l4": 16, "l5": 1, "gr": 16,
}


def dot(a, b):
    return jnp.dot(a, b, preferred_element_type=F32)


def dot_nt(a, b):
    return lax.dot_general(a, b, (((1,), (1,)), ((), ())), preferred_element_type=F32)


def dot_tn(a, b):
    return lax.dot_general(a, b, (((0,), (0,)), ((), ())), preferred_element_type=F32)


def gelu_pair(v):
    cdf = 0.5 * (1.0 + lax.erf(v * (1.0 / math.sqrt(2.0))))
    return v * cdf, cdf + v * jnp.exp(-0.5 * v * v) * (1.0 / math.sqrt(2.0 * math.pi))


def split(v):
    high = v.astype(BF16)
    return high, (v - high.astype(F32)).astype(BF16)


def body(*refs):
    taken = iter(refs)
    given = {name: next(taken) for name in INPUTS}
    handed = {name: next(taken) for name in HANDED}
    r = SimpleNamespace()
    for name in (*INPUTS, *HANDED, *SCRATCH):
        setattr(r, name, next(taken))
    sems = {name: (next(taken), next(taken)) for name in SEMS}
    fetch_sems, hand_sems = next(taken), next(taken)
    fetches = {
        name: pltpu.make_async_copy(given[name], getattr(r, name), fetch_sems.at[k])
        for k, name in enumerate(INPUTS)
    }
    for copy in fetches.values():
        copy.start()
    handing = []

    def fetched(*wanted):
        for name in wanted:
            fetches[name].wait()

    def hand(name):
        at = list(HANDED).index(name)
        copy = pltpu.make_async_copy(getattr(r, name), handed[name], hand_sems.at[at])
        copy.start()
        handing.append(copy)

    t = lax.axis_index("text")
    g = lax.axis_index("graph")
    c = lax.rem(t, 2)
    y = lax.div(t, 2)
    sib = t + 1 - 2 * c

    def at_y(step):
        return lax.rem(y + step, 4) * 2 + c

    up, opp, down = at_y(1), at_y(2), at_y(3)
    x, z = lax.div(g, 4), lax.rem(g, 4)

    def at_x(step):
        return lax.rem(x + step, 4)

    def at_z(step):
        return lax.rem(z + step, 4)

    ahead = lax.rem(g + 1, NG)
    behind = lax.rem(g + NG - 1, NG)
    pending = []

    def send(src, dst, kind, tag, to, start=True):
        copy = pltpu.make_async_remote_copy(
            src_ref=src, dst_ref=dst, send_sem=sems[kind][0].at[tag],
            recv_sem=sems[kind][1].at[tag], device_id=to, device_id_type=MESH,
        )
        if start:
            copy.start()
            pending.append(copy)
        return copy

    def arrived(dst, kind, tag):
        send(dst, dst, kind, tag, (sib, g), start=False).wait_recv()

    def each_peer(fn):
        def step(k, carry):
            fn(k, lax.rem(g + k, NG), lax.rem(g + NG - k, NG))
            return carry

        lax.fori_loop(1, NG, step, 0)

    def scatter(src_of, dst, kind):
        def one(k, to, source):
            pltpu.make_async_remote_copy(
                src_ref=src_of(to), dst_ref=dst.at[g], send_sem=sems[kind][0].at[k],
                recv_sem=sems[kind][1].at[k], device_id=(t, to), device_id_type=MESH,
            ).start()

        each_peer(one)

    def scatter_wait(dst, kind):
        each_peer(lambda k, to, source: arrived(dst.at[source], kind, k))

    def scatter_sent(src, kind):
        def one(k, to, source):
            send(src, src, kind, k, (t, to), start=False).wait_send()

        each_peer(one)

    barrier = pltpu.get_barrier_semaphore()

    def greet(to):
        pl.semaphore_signal(barrier, inc=1, device_id=to, device_id_type=MESH)

    for peer in (sib, up, opp, down):
        greet((peer, g))
    each_peer(lambda k, to, source: greet((t, to)))

    fetched("w_in", "w_out", "states")

    def halves(rows):
        return jnp.concatenate([rows[:, : D // 2], rows[:, D // 2 :]], axis=0)

    def joined(rows):
        return jnp.concatenate([rows[:OWN], rows[OWN:]], axis=1)

    r.pack_in[g] = halves(r.w_in[...].astype(F32)).astype(BF16)
    r.pack_out[z * 4 + x] = halves(r.w_out[...].astype(F32)).astype(BF16)

    for i in range(4):
        own = r.states[i * SEQ : (i + 1) * SEQ, :].astype(F32)
        r.smean[i : i + 1, :] = jnp.sum(own, axis=0, keepdims=True) * (1.0 / SEQ)
        mean = jnp.mean(own, axis=1, keepdims=True)
        centered = own - mean
        var = jnp.mean(centered * centered, axis=1, keepdims=True)
        r.normed[t, i * SEQ : (i + 1) * SEQ, :] = (centered * lax.rsqrt(var + 1e-05)).astype(BF16)
    fetched("table", "sf", "nf")
    for i in range(4):
        rows = slice(i * 256, (i + 1) * 256)
        nodes = r.table[rows, :]
        r.tn[RIM + i * 256 : RIM + (i + 1) * 256, :] = dot(nodes, r.nf[...]).astype(BF16)
        r.tself[rows, :] = dot(nodes, r.sf[...])

    pl.semaphore_wait(barrier, 19)
    own_in, own_out = r.pack_in.at[g], r.pack_out.at[z * 4 + x]
    for step in (1, 3, 2):
        send(own_in, own_in, "wi", step, (t, x * 4 + at_z(step)))
        send(own_out, own_out, "wo", step, (t, at_x(step) * 4 + z))
    mine = r.normed.at[t]
    send(mine, mine, "st", 0, (sib, g))
    low_half, high_half = mine.at[:128], mine.at[128:]
    send(low_half, low_half, "st", 1, (up, g))
    send(high_half, high_half, "st", 2, (down, g))
    send(high_half, high_half, "st", 9, (up, g))
    send(low_half, low_half, "st", 10, (down, g))

    fetched("adj", "src")
    def tiles(b, carry):
        rows = pl.ds(pl.multiple_of(b * 128, 128), 128)
        plain = [r.adj[b * 4 + k] for k in range(4)]
        turned = [p.astype(F32).T.astype(BF16) for p in plain]
        here = lax.broadcasted_iota(jnp.int32, (4, 8), 1) == b
        source = jnp.sum(jnp.where(here, r.src[...].astype(F32), 0.0), axis=1, keepdims=True)
        for s in range(12):
            hits = jnp.where(source == float(s), 1.0, 0.0)
            own = jnp.zeros((128, 128), BF16)
            other = jnp.zeros((128, 128), BF16)
            for k in range(4):
                hit = jnp.broadcast_to(hits[k : k + 1, :], (128, 128)).astype(BF16)
                own = own + plain[k] * hit
                other = other + turned[k] * hit
            r.e[rows, s * 128 : (s + 1) * 128] = own
            r.et[s * 128 : (s + 1) * 128, rows] = other
        return carry

    lax.fori_loop(0, 8, tiles, 0)

    for step in (1, 2, 3):
        arrived(r.pack_in.at[x * 4 + at_z(4 - step)], "wi", step)
    slab = r.pack_in.at[pl.ds(x * 4, 4)]
    for step in (1, 3, 2):
        send(slab, slab, "wi", 4 + step, (t, at_x(step) * 4 + z))
    for step in (1, 2, 3):
        arrived(r.pack_out.at[z * 4 + at_x(4 - step)], "wo", step)
    slab = r.pack_out.at[pl.ds(z * 4, 4)]
    for step in (1, 3, 2):
        send(slab, slab, "wo", 4 + step, (t, x * 4 + at_z(step)))

    fetched("ups", "ss", "ns")
    for i in (0, 5, 1, 2, 3, 4):
        rows = slice(i * 256, (i + 1) * 256)
        r.b2[rows, :] = dot(r.et[rows, :], r.ups[...])

    fetched("ids")
    row = lax.broadcasted_iota(jnp.int32, (NFT, NFT), 0)
    col = lax.broadcasted_iota(jnp.int32, (NFT, NFT), 1)
    wanted = (col & 256) + ((col >> 2) & 3) * 64 + ((col >> 4) & 15) * 4 + (col & 3)
    moved = jnp.where(row == wanted, 1.0, 0.0).astype(BF16)
    ids = jnp.broadcast_to(r.ids[...], (8, NFT))
    pieces = [((ids >> shift) & 63).astype(F32).astype(BF16) for shift in (0, 6, 12)]
    low, middle, high = [dot(p, moved) for p in pieces]
    spot = low + 64.0 * middle + 4096.0 * high
    spot_row = spot[:1, :]
    spot_col = jnp.broadcast_to(spot_row, (128, NFT)).T
    device = t * NG + g
    starts = [(t * NG + behind) * ROWS + 768 + e * 128 for e in range(2)]
    starts += [device * ROWS + e * 128 for e in range(8)]
    starts += [(t * NG + ahead) * ROWS + e * 128 for e in range(2)]
    for e in range(12):
        start = starts[e].astype(F32)
        down_rows = lax.broadcasted_iota(jnp.int32, (128, NFT), 0).astype(F32) + start
        hit = jnp.where(down_rows == spot_row, 1.0, 0.0)
        r.oh[e * 128 : (e + 1) * 128, :] = hit.astype(BF16)
        r.keep[e * 128 : (e + 1) * 128, :] = 1.0 - jnp.sum(hit, axis=1, keepdims=True)
        across = lax.broadcasted_iota(jnp.int32, (NFT, 128), 1).astype(F32) + start
        r.oht[:, e * 128 : (e + 1) * 128] = jnp.where(across == spot_col, 1.0, 0.0).astype(BF16)

    from_down, from_up, far = r.normed.at[down], r.normed.at[up], r.normed.at[opp]
    arrived(from_down.at[:128], "st", 1)
    send(from_down.at[:128], from_down.at[:128], "st", 3, (up, g))
    arrived(from_up.at[128:], "st", 2)
    send(from_up.at[128:], from_up.at[128:], "st", 4, (down, g))

    def unpack(packed, out, place):
        def step(k, carry):
            rows = pl.ds(pl.multiple_of(k * OWN, 8), OWN)
            r.wide[rows, :] = joined(packed[place(k)].astype(F32))
            return carry

        lax.fori_loop(0, NG, step, 0)
        out[...] = r.wide[...].astype(BF16)

    for step in (1, 2, 3):
        arrived(r.pack_in.at[pl.ds(at_x(4 - step) * 4, 4)], "wi", 4 + step)
    unpack(r.pack_in, r.wi, lambda k: k)

    def encode(slot):
        r.before[...] = dot_nt(r.normed[slot], r.wi[...])

        def node(i, carry):
            rows = pl.ds(pl.multiple_of(i * SEQ, SEQ), SEQ)
            value, slope = gelu_pair(r.before[rows, :])
            r.slope[slot, rows, :] = slope
            r.asum[pl.ds(slot * 4 + i, 1), :] = jnp.sum(value, axis=0, keepdims=True)
            return carry

        lax.fori_loop(0, 4, node, 0)

    def fellow(slot):
        return slot + 1 - 2 * c

    encode(t)
    arrived(r.normed.at[sib], "st", 0)
    encode(sib)
    arrived(from_down.at[128:], "st", 9)
    send(from_down, from_down, "st", 5, (sib, g))
    arrived(from_up.at[:128], "st", 10)
    send(from_up, from_up, "st", 6, (sib, g))
    encode(down)
    send(r.tn.at[RIM : 2 * RIM], r.tn.at[RIM + ROWS :], "rim", 0, (t, behind))
    send(r.tn.at[ROWS : ROWS + RIM], r.tn.at[:RIM], "rim", 1, (t, ahead))
    r.b2out[0] = r.b2[:RIM, :].astype(BF16)
    r.b2out[1] = r.b2[RIM + ROWS :, :].astype(BF16)
    send(r.b2out.at[0], r.b2in.at[1], "rim", 2, (t, behind))
    send(r.b2out.at[1], r.b2in.at[0], "rim", 3, (t, ahead))
    encode(up)
    arrived(r.normed.at[fellow(down)], "st", 5)
    encode(fellow(down))
    arrived(far.at[:128], "st", 3)
    send(far.at[:128], far.at[:128], "st", 7, (sib, g))
    arrived(far.at[128:], "st", 4)
    send(far.at[128:], far.at[128:], "st", 8, (sib, g))
    arrived(r.normed.at[fellow(up)], "st", 6)
    encode(fellow(up))
    encode(opp)
    far_pair = r.normed.at[fellow(opp)]
    arrived(far_pair.at[:128], "st", 7)
    arrived(far_pair.at[128:], "st", 8)
    encode(fellow(opp))

    for step in (1, 2, 3):
        arrived(r.pack_out.at[pl.ds(at_z(4 - step) * 4, 4)], "wo", 4 + step)
    unpack(r.pack_out, r.wo, lambda k: (k % 4) * 4 + k // 4)
    a_high, a_low = split(r.asum[...] * (1.0 / SEQ))
    r.part[...] = dot(a_high, r.wo[...]) + dot(a_low, r.wo[...])
    for i in range(4):
        spot_rows = pl.ds(t * 4 + i, 1)
        r.part[spot_rows, :] = r.part[spot_rows, :] + r.smean[i : i + 1, :]
    r.part2[0] = r.part[:16, :]
    r.part2[1] = r.part[16:, :]
    send(r.part2.at[1 - c], r.pairin, "pair", 0, (sib, g))
    arrived(r.pairin, "pair", 0)
    r.yemb[y] = (r.part2[c] + r.pairin[...]).astype(BF16)
    for step, peer in ((1, up), (2, opp), (3, down)):
        send(r.yemb.at[y], r.yemb.at[y], "ye", step, (peer, g))
    for step in (1, 2, 3):
        arrived(r.yemb.at[lax.rem(y + 4 - step, 4)], "ye", step)
    total = r.yemb[0].astype(F32) + r.yemb[1].astype(F32)
    total = total + r.yemb[2].astype(F32) + r.yemb[3].astype(F32)
    r.emb[c, g] = total.astype(BF16)

    def emb_out(k, to, source):
        ref = r.emb.at[c, g]
        send(ref, ref, "eg", k, (t, to), start=False).start()

    each_peer(emb_out)
    own_emb = r.emb.at[c, g]
    send(own_emb, own_emb, "es", 0, (sib, g))

    r.spread[...] = jnp.zeros_like(r.spread)
    r.spread[pl.ds(pl.multiple_of(lax.rem(g, 4) * 32, 32), 32), :] = r.asum[...]
    r.turned[...] = r.spread[...].T
    my_units = pl.ds(pl.multiple_of(g * OWN, 8), OWN)
    r.acols[g] = r.turned[my_units, :]

    arrived(r.b2in.at[0], "rim", 3)
    arrived(r.b2in.at[1], "rim", 2)
    r.b2[RIM : 2 * RIM, :] = r.b2[RIM : 2 * RIM, :] + r.b2in[0].astype(F32)
    r.b2[ROWS : ROWS + RIM, :] = r.b2[ROWS : ROWS + RIM, :] + r.b2in[1].astype(F32)
    r.back2[...] = r.b2[RIM : RIM + ROWS, :].astype(BF16)
    for i in range(4):
        rows = slice(i * 256, (i + 1) * 256)
        r.hg[rows, :] = dot_nt(r.ups[rows, :], r.ss[...]) + dot_nt(r.back2[rows, :], r.ns[...])
    arrived(r.tn.at[RIM + ROWS :], "rim", 0)
    arrived(r.tn.at[:RIM], "rim", 1)

    def emb_on(k, to, source):
        ref = r.emb.at[c, source]
        arrived(ref, "eg", k)
        send(ref, ref, "es", k, (sib, g), start=False).start()

    each_peer(emb_on)
    arrived(r.emb.at[1 - c, g], "es", 0)
    each_peer(lambda k, to, source: arrived(r.emb.at[1 - c, source], "es", k))

    scatter(lambda to: r.turned.at[pl.ds(pl.multiple_of(to * OWN, 8), OWN)], r.acols, "ac")

    emb_all = r.emb[...].reshape(NFT, D)
    r.embproj[:, :HID] = dot(emb_all, r.sf[...]).astype(BF16)
    r.embproj[:, HID:] = dot(emb_all, r.nf[...]).astype(BF16)
    for i in range(6):
        rows = slice(i * 256, (i + 1) * 256)
        new = dot(r.oh[rows, :], r.embproj[:, HID:])
        r.pn[rows, :] = (r.tn[rows, :].astype(F32) * r.keep[rows, :] + new).astype(BF16)

    for i in range(4):
        rows = slice(i * 256, (i + 1) * 256)
        ext = slice(RIM + i * 256, RIM + (i + 1) * 256)
        pre = r.tself[rows, :] * r.keep[ext, :] + dot(r.oh[ext, :], r.embproj[:, :HID])
        pre = pre + dot(r.e[rows, :], r.pn[...])
        value, slope = gelu_pair(pre)
        r.hid[ext, :] = value.astype(BF16)
        r.fb[rows, :HID] = (r.hg[rows, :] * slope).astype(BF16)
    def over_peers(ref):
        total = ref[0].astype(F32)
        for k in range(1, NG):
            total = total + ref[k].astype(F32)
        return total

    def over_y(ref):
        return (ref[0].astype(F32) + ref[1].astype(F32)) + (ref[2].astype(F32) + ref[3].astype(F32))

    def features(i):
        rows = slice(i * 256, (i + 1) * 256)
        ext = slice(RIM + i * 256, RIM + (i + 1) * 256)
        old = r.table[rows, :].astype(F32) * r.keep[ext, :]
        r.feat[rows, :] = (old + dot(r.oh[ext, :], emb_all)).astype(BF16)

    for i in range(4):
        features(i)

    def keep_grad(buffer, first, left, right):
        for q in range(left.shape[1] // 256):
            term = dot_tn(left[:, q * 256 : (q + 1) * 256], right) * NODE_SCALE
            at = slice(first + q * 16, first + q * 16 + 16)
            for side in range(2):
                cols = slice(side * 128, (side + 1) * 128)
                buffer[side, at] = term[:, cols].astype(BF16).reshape(16, 16, 128)

    hidden = r.hid[RIM : RIM + ROWS, :]
    keep_grad(r.e0, 48, hidden, r.ups[...])
    keep_grad(r.e0, 64, hidden, r.back2[...])
    keep_grad(r.e0, 0, r.feat, r.fb[:, :HID])
    send(r.e0.at[1 - c], r.e1in, "e1", 0, (sib, g))

    for i in (0, 5, 1, 2, 3, 4):
        rows = slice(i * 256, (i + 1) * 256)
        term = dot(r.et[rows, :], r.fb[:, :HID])
        r.b1[rows, :] = term
        r.b1b[rows, :] = term.astype(BF16)

    for i in range(2):
        rows = slice(i * 256, (i + 1) * 256)
        first = dot(r.oht[rows, RIM : RIM + ROWS], r.fb[:, :HID]).astype(BF16)
        back = dot(r.oht[rows, :], r.b1b[...]).astype(BF16)
        r.pick[i, :, :, :HID] = first.reshape(NG, 16, HID)
        r.pick[i, :, :, HID:] = back.reshape(NG, 16, HID)
    send(r.pick.at[1 - c], r.pickin, "pk", 0, (sib, g))


    arrived(r.e1in, "e1", 0)
    r.e1[...] = (r.e0[c].astype(F32) + r.e1in[...].astype(F32)).astype(BF16)
    r.e2[y] = r.e1[pl.ds(y * 20, 20)]
    for step in (1, 3, 2):
        to_y = lax.rem(y + step, 4)
        send(r.e1.at[pl.ds(to_y * 20, 20)], r.e2.at[y], "e2", step, (to_y * 2 + c, g))
    arrived(r.pickin, "pk", 0)
    r.pick1[...] = (r.pick[c].astype(F32) + r.pickin[...].astype(F32)).astype(BF16)
    r.pickg[g] = r.pick1[g]
    scatter(lambda to: r.pick1.at[to], r.pickg, "pg")
    send(r.b1b.at[:RIM], r.b1in.at[1], "rim", 6, (t, behind))
    send(r.b1b.at[RIM + ROWS :], r.b1in.at[0], "rim", 7, (t, ahead))

    scatter_wait(r.pickg, "pg")
    r.picky[y] = over_peers(r.pickg).astype(BF16)
    for step, peer in ((1, up), (2, opp), (3, down)):
        send(r.picky.at[y], r.picky.at[y], "py", step, (peer, g))
    for step in (1, 2, 3):
        arrived(r.e2.at[lax.rem(y + 4 - step, 4)], "e2", step)
    r.e3out[...] = over_y(r.e2).astype(BF16)

    def piece_out(k, to, source):
        @pl.when(to < 10)
        def _():
            send(r.e3out.at[pl.ds(to * 2, 2)], r.e3.at[g], "e3", k, (t, to), start=False).start()

    each_peer(piece_out)


    arrived(r.b1in.at[0], "rim", 7)
    arrived(r.b1in.at[1], "rim", 6)
    r.b1[RIM : 2 * RIM, :] = r.b1[RIM : 2 * RIM, :] + r.b1in[0].astype(F32)
    r.b1[ROWS : ROWS + RIM, :] = r.b1[ROWS : ROWS + RIM, :] + r.b1in[1].astype(F32)
    r.fb[:, HID:] = r.b1[RIM : RIM + ROWS, :].astype(BF16)
    hand("fb")
    keep_grad(r.l0, 0, r.feat, r.fb[:, HID:])
    send(r.l0.at[1 - c], r.l1in, "l1", 0, (sib, g))

    for step in (1, 2, 3):
        arrived(r.picky.at[lax.rem(y + 4 - step, 4)], "py", step)
    r.pickall[g, c] = over_y(r.picky).astype(BF16)
    own_picks = r.pickall.at[g, c]
    send(own_picks, own_picks, "ps", 0, (sib, g))

    def picks_out(k, to, source):
        send(own_picks, own_picks, "ag", k, (t, to), start=False).start()

    each_peer(picks_out)
    arrived(r.l1in, "l1", 0)
    r.l1[...] = (r.l0[c].astype(F32) + r.l1in[...].astype(F32)).astype(BF16)
    r.l2[g] = r.l1[pl.ds(g * 3, 3)]
    scatter(lambda to: r.l1.at[pl.ds(to * 3, 3)], r.l2, "l2")
    send(r.hid.at[RIM : 2 * RIM], r.hid.at[RIM + ROWS :], "rim", 4, (t, behind))
    send(r.hid.at[ROWS : ROWS + RIM], r.hid.at[:RIM], "rim", 5, (t, ahead))

    arrived(r.pickall.at[g, 1 - c], "ps", 0)
    rows32 = r.pickall[g].reshape(32, 2 * HID)

    def node_grads(rows):
        return dot_nt(rows[:, :HID], r.sf[...]) + dot_nt(rows[:, HID:], r.nf[...])

    node_grad = node_grads(rows32)
    r.nodeg[...] = node_grad
    for i in range(4):
        r.ngrad[i : i + 1, :] = r.nodeg[pl.ds(t * 4 + i, 1), :]
    hand("ngrad")
    small = (node_grad * (1.0 / SEQ)).astype(BF16)
    r.act[...] = dot_nt(small, r.wo[...])

    def pre_grad(n, carry):
        slot = n // 4
        rows = pl.ds(pl.multiple_of((n % 4) * SEQ, SEQ), SEQ)
        r.pre[slot, rows, :] = (r.act[pl.ds(n, 1), :] * r.slope[slot, rows, :]).astype(BF16)
        return carry

    lax.fori_loop(0, 32, pre_grad, 0)

    @pl.when(g < 10)
    def _():
        r.e3[g] = r.e3out[pl.ds(g * 2, 2)]
        scatter_wait(r.e3, "e3")
        r.early[c, y, pl.ds(g * 2, 2)] = over_peers(r.e3).astype(BF16)
        own = r.early.at[c, y, pl.ds(g * 2, 2)]

        def early_out(k, to, source):
            send(own, own, "e4", k, (t, to), start=False).start()

        each_peer(early_out)

    pre_all = r.pre[...].reshape(NT * 256, CHUNK)
    norm_all = r.normed[...].reshape(NT * 256, D)
    for i in range(3):
        cols = slice(i * 128, (i + 1) * 128)
        r.gfull[cols, :] = dot_tn(pre_all[:, cols], norm_all) * TEXT_SCALE

    def pack(k, carry):
        rows = pl.ds(pl.multiple_of(k * OWN, 8), OWN)
        r.gpack[k] = halves(r.gfull[rows, :]).astype(BF16)
        return carry

    lax.fori_loop(0, NG, pack, 0)
    r.grecv[g] = r.gpack[g]
    scatter(lambda to: r.gpack.at[to], r.grecv, "gr")

    scatter_wait(r.l2, "l2")
    r.l3[y] = over_peers(r.l2).astype(BF16)
    for step, peer in ((1, up), (2, opp), (3, down)):
        send(r.l3.at[y], r.l3.at[y], "l3", step, (peer, g))

    def picks_on(k, to, source):
        ref = r.pickall.at[source, c]
        arrived(ref, "ag", k)
        send(ref, ref, "as", k, (sib, g), start=False).start()

    each_peer(picks_on)

    def early_in(k, to, source):
        @pl.when(source < 10)
        def _():
            arrived(r.early.at[c, y, pl.ds(source * 2, 2)], "e4", k)

    each_peer(early_in)
    own_quarter = r.early.at[c, y]
    for step, peer in ((1, up), (3, down), (2, opp)):
        send(own_quarter, own_quarter, "e5", step, (peer, g))

    for step in (1, 2, 3):
        arrived(r.l3.at[lax.rem(y + 4 - step, 4)], "l3", step)
    r.late[c, pl.ds(g * 3, 3)] = over_y(r.l3).astype(BF16)
    own_late = r.late.at[c, pl.ds(g * 3, 3)]

    def late_out(k, to, source):
        send(own_late, own_late, "l4", k, (t, to), start=False).start()

    each_peer(late_out)


    arrived(r.hid.at[RIM + ROWS :], "rim", 4)
    arrived(r.hid.at[:RIM], "rim", 5)
    for i in range(6):
        rows = slice(i * 256, (i + 1) * 256)
        r.proj2[rows, :] = dot(r.hid[rows, :], r.ns[...]).astype(BF16)
    for i in range(4):
        rows = slice(i * 256, (i + 1) * 256)
        ext = slice(RIM + i * 256, RIM + (i + 1) * 256)
        r.gnn[rows, :] = (dot(r.hid[ext, :], r.ss[...]) + dot(r.e[rows, :], r.proj2[...])).astype(BF16)
    hand("gnn")


    scatter_wait(r.acols, "ac")
    each_peer(lambda k, to, source: arrived(r.pickall.at[source, 1 - c], "as", k))
    small_all = (node_grads(r.pickall[...].reshape(NFT, 2 * HID)) * (1.0 / SEQ)).astype(BF16)
    units = jnp.zeros((OWN, D), F32)
    for q in range(4):
        lanes = (r.acols[4 * q] + r.acols[4 * q + 1]) + (r.acols[4 * q + 2] + r.acols[4 * q + 3])
        a_high, a_low = split(lanes)
        block = small_all[q * 128 : (q + 1) * 128]
        units = units + (dot(a_high, block) + dot(a_low, block))
    r.gout[...] = units * TEXT_SCALE
    hand("gout")


    for step in (1, 2, 3):
        arrived(r.early.at[c, lax.rem(y + 4 - step, 4)], "e5", step)
    send(r.early.at[c], r.early.at[c], "e6", 0, (sib, g))
    each_peer(lambda k, to, source: arrived(r.late.at[c, pl.ds(source * 3, 3)], "l4", k))
    send(r.late.at[c], r.late.at[c], "l5", 0, (sib, g))


    scatter_wait(r.grecv, "gr")
    r.gin[...] = joined(over_peers(r.grecv))
    hand("gin")

    arrived(r.late.at[1 - c], "l5", 0)
    hand("late")
    arrived(r.early.at[1 - c], "e6", 0)
    hand("early")

    for copy in pending:
        copy.wait_send()
    scatter_sent(own_emb, "eg")
    each_peer(lambda k, to, source: send(own_emb, own_emb, "es", k, (sib, g), start=False).wait_send())
    scatter_sent(r.acols.at[0], "ac")
    scatter_sent(r.pick1.at[0], "pg")
    scatter_sent(own_picks, "ag")
    each_peer(lambda k, to, source: send(own_picks, own_picks, "as", k, (sib, g), start=False).wait_send())
    scatter_sent(r.gpack.at[0], "gr")
    scatter_sent(r.l2.at[0], "l2")
    scatter_sent(own_late, "l4")

    def piece_sent(k, to, source):
        @pl.when(to < 10)
        def _():
            send(r.e3.at[0], r.e3.at[0], "e3", k, (t, to), start=False).wait_send()

    each_peer(piece_sent)

    @pl.when(g < 10)
    def _():
        scatter_sent(r.e3.at[0], "e4")

    for copy in handing:
        copy.wait()


FINISH = {
    "fb": ((ROWS, 2 * HID), BF16),
    "sf": ((D, HID), BF16),
    "nf": ((D, HID), BF16),
    "early": ((2, 80, 16, 128), BF16),
    "late": ((2, 48, 16, 128), BF16),
    "gnn": ((ROWS, HID), BF16),
    "ngrad": ((4, D), F32),
    "gin": ((OWN, D), F32),
    "gout": ((OWN, D), F32),
}
RESULTS = {
    "gnn": ((ROWS, HID), BF16),
    "tgrad": ((ROWS, D), F32),
    "ngrad": ((4, D), F32),
    "gin": ((OWN, D), F32),
    "gout": ((OWN, D), F32),
    "gsf": ((D, HID), F32),
    "gnf": ((D, HID), F32),
    "gss": ((HID, HID), F32),
    "gns": ((HID, HID), F32),
}
MADE = ("tgrad", "gsf", "gnf", "gss", "gns")


def finish(*refs):
    taken = iter(refs)
    given = {name: next(taken) for name in FINISH}
    out = {name: next(taken) for name in RESULTS}
    r = SimpleNamespace(**{name: next(taken) for name in (*FINISH, *MADE)})
    in_sems, out_sems = next(taken), next(taken)
    leaving = []
    fetches = {
        name: pltpu.make_async_copy(given[name], getattr(r, name), in_sems.at[k])
        for k, name in enumerate(FINISH)
    }
    for copy in fetches.values():
        copy.start()
    def leave(source, target, at):
        copy = pltpu.make_async_copy(source, target, out_sems.at[at])
        copy.start()
        leaving.append(copy)

    for name in ("fb", "sf", "nf"):
        fetches[name].wait()
    for i in range(4):
        rows = slice(i * 256, (i + 1) * 256)
        r.tgrad[rows, :] = dot_nt(r.fb[rows, :HID], r.sf[...]) + dot_nt(r.fb[rows, HID:], r.nf[...])
        leave(r.tgrad.at[rows], out["tgrad"].at[rows], i)
    for name in ("early", "late"):
        fetches[name].wait()
    for c in range(2):
        cols = slice(c * 128, (c + 1) * 128)
        r.gsf[:, cols] = r.early[c, :48].astype(F32).reshape(D, 128)
        r.gss[:, cols] = r.early[c, 48:64].astype(F32).reshape(HID, 128)
        r.gns[:, cols] = r.early[c, 64:].astype(F32).reshape(HID, 128)
        r.gnf[:, cols] = r.late[c].astype(F32).reshape(D, 128)
    for k, name in enumerate(MADE[1:]):
        leave(getattr(r, name), out[name], 4 + k)
    for k, name in enumerate(("gnn", "ngrad", "gin", "gout")):
        fetches[name].wait()
        leave(getattr(r, name), out[name], 8 + k)
    for copy in leaving:
        copy.wait()


def per_device(states, w_in, w_out, table, adj, sources, node_ids, sf, nf, ss, ns, ups):
    anywhere = pl.BlockSpec(memory_space=pl.ANY)
    scratch = []
    for kind in (INPUTS, HANDED, SCRATCH):
        scratch += [pltpu.VMEM(shape, dtype) for shape, dtype in kind.values()]
    for count in SEMS.values():
        scratch += [pltpu.SemaphoreType.DMA((count,)), pltpu.SemaphoreType.DMA((count,))]
    scratch += [pltpu.SemaphoreType.DMA((len(INPUTS),)), pltpu.SemaphoreType.DMA((len(HANDED),))]
    gnn, fb, early, late, ngrad, gin, gout = pl.pallas_call(
        body,
        out_shape=tuple(jax.ShapeDtypeStruct(*spec) for spec in HANDED.values()),
        in_specs=[anywhere] * len(INPUTS),
        out_specs=tuple([anywhere] * len(HANDED)),
        scratch_shapes=scratch,
        compiler_params=pltpu.CompilerParams(
            collective_id=0, has_side_effects=True, vmem_limit_bytes=62 * 1024 * 1024
        ),
    )(
        states.reshape(4 * SEQ, D), w_in, w_out, node_ids.reshape(1, NFT), sources.T,
        adj.reshape(32, 128, 128), ups, table, sf, nf, ss, ns,
    )

    scratch = [pltpu.VMEM(*spec) for spec in FINISH.values()]
    scratch += [pltpu.VMEM(*RESULTS[name]) for name in MADE]
    scratch += [pltpu.SemaphoreType.DMA((n,)) for n in (len(FINISH), 12)]
    return tuple(pl.pallas_call(
        finish,
        out_shape=[jax.ShapeDtypeStruct(*spec) for spec in RESULTS.values()],
        in_specs=[anywhere] * len(FINISH),
        out_specs=[anywhere] * len(RESULTS),
        scratch_shapes=scratch,
        compiler_params=pltpu.CompilerParams(vmem_limit_bytes=62 * 1024 * 1024),
    )(fb, sf, nf, early.reshape(2, 80, 16, 128), late, gnn, ngrad, gin, gout))


def solution(mesh):
    both = ("text", "graph")
    rows = P(both, None)
    return jax.shard_map(
        per_device,
        mesh=mesh,
        in_specs=(
            P(both, None, None), rows, rows, rows, P(both, None, None, None), rows,
            P(), P(), P(), P(), P(), rows,
        ),
        out_specs=(rows, rows, rows, rows, rows, P(), P(), P(), P()),
        check_vma=False,
    )
```
